32 devices in a mesh: seq: 8 (over z, y), head: 4 (over x, core).
Axes of the slice: x: 2, y: 2, z: 4, core: 2. Of those that a mesh axis runs over, the one named last changes fastest.
Arguments:
- queries: bfloat16 [8192, 2048], P('seq', 'head'), may hold values from -11 to 11
- keys_values: bfloat16 [8192, 2, 2048], P('seq', None, 'head'), may hold values from -6 to 6
- rand_blocks: int32 [128, 2], P('seq'), may hold values from 0 to 127, as said below
- w_out: bfloat16 [2048, 4096], P('head'), may hold values from -1 to 1
Outputs:
- mixed: bfloat16 [8192, 4096], P(('seq', 'head'))
The draws below stay inside these ranges and needn't reach their ends.
Inputs may be any that keep to these rules, and one draw needn't show every extreme that they name: `rand_blocks`: of the 32 entries in the rows of one index of seq, at most 4 name blocks o * 16 to o * 16 + 15 of any one index o; in every draw the blocks of some index o are named exactly 4 times from the rows of every index.
All inputs are finite; a program needn't handle non-finite values.
Results may differ from the reference program's by a relative error of at most 0.013.
Values may be sent and summed in bfloat16 or wider, within the bound.
A program may use at most 128 MiB of HBM per device.

```python
import jax
import jax.numpy as jnp
from jax import lax

D = 4096
HEADS = 16
HEAD_DIM = 128
BLOCK = 64
RAND = 2
BPD = 16
NB = 128
TOKENS = 8192
GROUPS = 4
FEAT = 2048
FEAT_GROUP = 512
N_SEQ = 8


def attention_inputs(key):
    base = jax.random.fold_in(key, 17)
    part_q, part_k, part_v = jax.random.split(base, 3)
    feat = HEADS * HEAD_DIM
    queries = jnp.clip(jax.random.normal(part_q, (TOKENS, feat), jnp.float32), -6.0, 6.0)
    keys = jnp.clip(jax.random.normal(part_k, (TOKENS, feat), jnp.float32), -6.0, 6.0)
    values = jnp.clip(jax.random.normal(part_v, (TOKENS, feat), jnp.float32), -6.0, 6.0)
    return (queries, jnp.stack([keys, values], axis=1))


def draw_queries(key, part):
    queries, paired = attention_inputs(key)
    return queries.astype(jnp.bfloat16)


def draw_keys_values(key, part):
    queries, paired = attention_inputs(key)
    return paired.astype(jnp.bfloat16)


def draw_rand_blocks(key, part):
    entries = RAND * BPD
    devices = N_SEQ
    star = jax.random.randint(jax.random.fold_in(key, 1), (), 0, devices)
    device_keys = jax.random.split(jax.random.fold_in(key, 2), devices)

    def one_device(sub):
        key_a, key_b, key_c = jax.random.split(sub, 3)
        others = (star + 1 + jax.random.permutation(key_a, devices - 1)) % devices
        order = jnp.concatenate([star[None], others])
        owners = order[jnp.arange(entries) % devices]
        owners = owners[jax.random.permutation(key_b, entries)]
        offsets = jax.random.randint(key_c, (entries,), 0, BPD)
        return (owners * BPD + offsets).astype(jnp.int32)
    blocks = jax.vmap(one_device)(device_keys)
    return blocks.reshape(NB, RAND)


def block_levels(own_key, extent, shards, smallest, top_value):
    loudness = 1.0
    for position, shards_of in shards:
        heights = jax.random.uniform(jax.random.fold_in(jax.random.fold_in(own_key, 6), position), (shards_of,), jnp.float32, smallest / len(shards), top_value / len(shards))
        loudness = loudness * jnp.repeat(jnp.exp(heights), extent[position] // shards_of).reshape((-1,) + (1,) * (len(extent) - 1 - position))
    return loudness


def normal_values(rng, extent, scale, bound, cuts=(), kind=jnp.bfloat16):
    result = jax.random.normal(rng, extent, jnp.float32) * scale
    if len(cuts) > 0:
        result = block_levels(rng, extent, cuts, -0.22, 0.18) * result
    return jnp.clip(result, min=-bound, max=bound).astype(kind)


def setup_inputs(seed: int = 0) -> dict:
    arg_keys = jax.random.split(jax.random.key(seed), 5)
    return {
        "queries": draw_queries(jax.random.fold_in(arg_keys[4], 71), 0),
        "keys_values": draw_keys_values(jax.random.fold_in(arg_keys[4], 71), 0),
        "rand_blocks": draw_rand_blocks(jax.random.fold_in(arg_keys[4], 71), 0),
        "w_out": normal_values(arg_keys[3], (FEAT, D), (FEAT // 64) ** -0.5, 1.0, ((0, 4),)),
    }


def reference(queries, keys_values, rand_blocks, w_out):
    scale = HEAD_DIM ** -0.5
    query_groups = queries.reshape(N_SEQ, BPD, BLOCK, HEADS, HEAD_DIM)
    block_kv = keys_values.reshape(NB, BLOCK, 2, HEADS, HEAD_DIM)
    rand_groups = rand_blocks.reshape(N_SEQ, BPD, RAND)
    block_ids = jnp.arange(NB, dtype=jnp.int32).reshape(N_SEQ, BPD)

    def one_group(item):
        query_part, rand_part, ids = item
        zeros_ids = jnp.zeros_like(ids)
        last_ids = zeros_ids + (NB - 1)
        taken = [ids - 1, ids, ids + 1, zeros_ids, last_ids]
        valid = [ids >= 1, ids >= 0, ids <= NB - 2, ids >= 2, ids <= NB - 3]
        for column in range(RAND):
            chosen = rand_part[:, column]
            clash = chosen == taken[0]
            for other in taken[1:]:
                clash = jnp.logical_or(clash, chosen == other)
            valid.append(jnp.logical_not(clash))
            taken.append(chosen)
        index = jnp.clip(jnp.stack(taken, axis=1), 0, NB - 1).astype(jnp.int32)
        mask = jnp.repeat(jnp.stack(valid, axis=1), BLOCK, axis=1)[:, None, None, :]
        picked = block_kv[index]
        count = index.shape[1] * BLOCK
        keys = picked[:, :, :, 0].reshape(BPD, count, HEADS, HEAD_DIM).astype(jnp.float32)
        values = picked[:, :, :, 1].reshape(BPD, count, HEADS, HEAD_DIM).astype(jnp.float32)
        scores = jnp.einsum("jqhd,jkhd->jhqk", query_part.astype(jnp.float32), keys) * scale
        scores = jnp.where(mask, scores, -1e30)
        peak = jnp.max(scores, axis=-1, keepdims=True)
        raw = jnp.where(mask, jnp.exp(scores - peak), 0.0)
        total = jnp.sum(raw, axis=-1)
        weights = raw.astype(jnp.bfloat16).astype(jnp.float32)
        mixture = jnp.einsum("jhqk,jkhd->jqhd", weights, values)
        attended = (mixture / jnp.transpose(total, (0, 2, 1))[..., None]).astype(jnp.bfloat16)
        attended = attended.reshape(BPD * BLOCK, FEAT)
        partials = []
        for group in range(GROUPS):
            lower = group * FEAT_GROUP
            term = jnp.dot(attended[:, lower:lower + FEAT_GROUP], w_out[lower:lower + FEAT_GROUP], preferred_element_type=jnp.float32)
            partials.append(term.astype(jnp.bfloat16))
        stacked = lax.optimization_barrier(jnp.stack(partials))
        return jnp.sum(stacked.astype(jnp.float32), axis=0).astype(jnp.bfloat16)

    mixed = lax.map(one_group, (query_groups, rand_groups, block_ids))
    return mixed.reshape(TOKENS, D)
```

```python
import functools
from functools import reduce

import jax
import jax.numpy as jnp
from jax import lax
from jax.experimental import pallas as pl
from jax.experimental.pallas import tpu as pltpu
from jax.sharding import PartitionSpec as P

HEAD_DIM = 128
BLOCK = 64
W_CHUNKS = 4
NEG = -1e30


def kernel(
    n,
    slots,
    blocks,
    heads,
    q_ref,
    kv_ref,
    tab_ref,
    slot_ref,
    bias_ref,
    w_ref,
    out_ref,
    kvp,
    ends,
    tabs,
    tabs_s,
    stage,
    recv,
    m_ref,
    l_ref,
    acc,
    att,
    attr,
    wall,
    oacc,
    tab_send,
    tab_recv,
    tab_local,
    halo_send,
    halo_recv,
    first_send,
    final_send,
    ends_recv,
    rand_send,
    rand_recv,
    w_local,
    wx_send,
    wx_recv,
    ws_send,
    ws_recv,
    wf_send,
    wf_recv,
    att_send,
    att_recv,
):
    me = lax.axis_index("seq")
    h = lax.axis_index("head")
    sib = h + 1 - 2 * lax.rem(h, 2)
    across = lax.rem(h + 2, 4)
    across_sib = lax.rem(sib + 2, 4)
    others = (across, across_sib, sib)
    total_blocks = n * blocks
    scale = HEAD_DIM ** (-0.5)
    w_rows = w_ref.shape[0] // W_CHUNKS
    feat = heads * HEAD_DIM

    def remote(src, dst, ssem, rsem, seq, head):
        return pltpu.make_async_remote_copy(
            src_ref=src,
            dst_ref=dst,
            send_sem=ssem,
            recv_sem=rsem,
            device_id=(seq, head),
            device_id_type=pl.DeviceIdType.MESH,
        )

    def peer(i):
        step = (i + 1) // 2
        d = n // 2 + step * (2 * lax.rem(i, 2) - 1)
        return lax.rem(me + d, n)

    barrier = pltpu.get_barrier_semaphore()

    def greet(i, c):
        pl.semaphore_signal(
            barrier, inc=1, device_id=(peer(i), h), device_id_type=pl.DeviceIdType.MESH
        )
        return c

    lax.fori_loop(0, n - 1, greet, 0)
    for g in others:
        pl.semaphore_signal(barrier, inc=1, device_id=(me, g), device_id_type=pl.DeviceIdType.MESH)
    pl.semaphore_wait(barrier, n - 1 + 3)

    def tab_copy(s, dest):
        return remote(
            tab_ref, tabs.at[pl.ds(s * 8, 8)], tab_send.at[dest], tab_recv.at[s], dest, h
        )

    def tab_start(i, c):
        tab_copy(me, peer(i)).start()
        return c

    lax.fori_loop(0, n - 1, tab_start, 0)

    def to_right():
        return remote(
            kv_ref.at[blocks - 1], kvp.at[0], halo_send.at[0], halo_recv.at[0], lax.rem(me + 1, n), h
        )

    def to_left():
        return remote(
            kv_ref.at[0],
            kvp.at[blocks + 1],
            halo_send.at[1],
            halo_recv.at[1],
            lax.rem(me + n - 1, n),
            h,
        )

    def first_copy(dest):
        return remote(kv_ref.at[0], ends.at[0], first_send.at[dest], ends_recv.at[0], dest, h)

    def final_copy(dest):
        return remote(kv_ref.at[blocks - 1], ends.at[1], final_send.at[dest], ends_recv.at[1], dest, h)

    @pl.when(me == 0)
    def _():
        def go(i, c):
            first_copy(peer(i)).start()
            return c

        lax.fori_loop(0, n - 1, go, 0)
        ends[0] = kv_ref[0]
        kvp[0] = jnp.zeros_like(kvp[0])

    @pl.when(me == n - 1)
    def _():
        def go(i, c):
            final_copy(peer(i)).start()
            return c

        lax.fori_loop(0, n - 1, go, 0)
        ends[1] = kv_ref[blocks - 1]
        kvp[blocks + 1] = jnp.zeros_like(kvp[0])

    @pl.when(me < n - 1)
    def _():
        to_right().start()

    @pl.when(me > 0)
    def _():
        to_left().start()

    def w_piece(g, c):
        return wall.at[g, pl.ds(c * w_rows, w_rows)]

    def wx_copy(g, c):
        return remote(
            w_ref.at[pl.ds(c * w_rows, w_rows)],
            w_piece(g, c),
            wx_send.at[c],
            wx_recv.at[c],
            me,
            across,
        )

    for c in range(W_CHUNKS):
        wx_copy(h, c).start()

    def tab_wait(i, c):
        tab_copy(peer(i), me).wait_recv()
        return c

    lax.fori_loop(0, n - 1, tab_wait, 0)
    tabs[pl.ds(pl.multiple_of(me * 8, 8), 8), :] = tab_ref[...]
    to_smem = pltpu.make_async_copy(tabs, tabs_s, tab_local)
    to_smem.start()
    to_smem.wait()

    def rand_copy(s, dest):
        return remote(stage.at[dest], recv.at[s], rand_send.at[dest], rand_recv.at[s], dest, h)

    def rand_start(i, c):
        dest = peer(i)
        for k in range(slots):
            stage[dest, k] = kv_ref[tabs_s[dest * 8, me * slots + k]]
        rand_copy(me, dest).start()
        return c

    lax.fori_loop(0, n - 1, rand_start, 0)
    for k in range(slots):
        recv[me, k] = kv_ref[tabs_s[me * 8, me * slots + k]]

    w_own = pltpu.make_async_copy(w_ref, wall.at[h], w_local)
    w_own.start()
    ws_copy = remote(w_ref, wall.at[h], ws_send, ws_recv, me, sib)
    ws_copy.start()

    def fill(j, c):
        kvp[j + 1] = kv_ref[j]
        return c

    lax.fori_loop(0, blocks, fill, 0)

    @pl.when(me > 0)
    def _():
        to_right().wait_recv()
        first_copy(me).wait_recv()

    @pl.when(me < n - 1)
    def _():
        to_left().wait_recv()
        final_copy(me).wait_recv()

    nt = (((1,), (1,)), ((), ()))

    def near(j, c):
        block = me * blocks + j
        rows = pl.ds(pl.multiple_of(j * BLOCK, BLOCK), BLOCK)
        b_prev = jnp.where(block >= 1, 0.0, NEG)
        b_next = jnp.where(block <= total_blocks - 2, 0.0, NEG)
        b_first = jnp.where(block >= 2, 0.0, NEG)
        b_final = jnp.where(block <= total_blocks - 3, 0.0, NEG)
        col = lax.broadcasted_iota(jnp.int32, (BLOCK, 3 * BLOCK), 1)
        b_win = jnp.where(col < BLOCK, b_prev, jnp.where(col >= 2 * BLOCK, b_next, 0.0))
        cole = lax.broadcasted_iota(jnp.int32, (BLOCK, 2 * BLOCK), 1)
        b_end = jnp.where(cole < BLOCK, b_first, b_final)
        for hd in range(heads):
            kc = pl.ds(hd * HEAD_DIM, HEAD_DIM)
            vc = pl.ds(feat + hd * HEAD_DIM, HEAD_DIM)
            qh = q_ref[rows, kc]
            kw = kvp[pl.ds(j, 3), :, kc].reshape(3 * BLOCK, HEAD_DIM)
            vw = kvp[pl.ds(j, 3), :, vc].reshape(3 * BLOCK, HEAD_DIM)
            ke = ends[:, :, kc].reshape(2 * BLOCK, HEAD_DIM)
            ve = ends[:, :, vc].reshape(2 * BLOCK, HEAD_DIM)
            sw = lax.dot_general(qh, kw, nt, preferred_element_type=jnp.float32) * scale + b_win
            se = lax.dot_general(qh, ke, nt, preferred_element_type=jnp.float32) * scale + b_end
            m = jnp.maximum(
                jnp.max(sw, axis=1, keepdims=True), jnp.max(se, axis=1, keepdims=True)
            )
            pw = jnp.exp(sw - m)
            pe = jnp.exp(se - m)
            tot = jnp.sum(pw, axis=1, keepdims=True) + jnp.sum(pe, axis=1, keepdims=True)
            o = jnp.dot(pw.astype(jnp.bfloat16), vw, preferred_element_type=jnp.float32)
            o = o + jnp.dot(pe.astype(jnp.bfloat16), ve, preferred_element_type=jnp.float32)
            m_ref[rows, kc] = jnp.broadcast_to(m, (BLOCK, HEAD_DIM))
            l_ref[rows, kc] = jnp.broadcast_to(tot, (BLOCK, HEAD_DIM))
            acc[rows, kc] = o
        return c

    lax.fori_loop(0, blocks, near, 0)

    def wf_copy(g, c):
        return remote(w_piece(g, c), w_piece(g, c), wf_send.at[c], wf_recv.at[c], me, sib)

    def forward(c):
        wx_copy(across, c).wait_recv()
        wf_copy(across, c).start()

    for c in range(W_CHUNKS - 1):
        forward(c)

    def rand_wait(i, c):
        rand_copy(peer(i), me).wait_recv()
        return c

    lax.fori_loop(0, n - 1, rand_wait, 0)

    quarter = blocks // 4

    def far(t):
        def one(u, c):
            j = t * quarter + u
            rows = pl.ds(pl.multiple_of(j * BLOCK, BLOCK), BLOCK)
            urows = pl.ds(pl.multiple_of(u * BLOCK, BLOCK), BLOCK)
            s0 = slot_ref[2 * j]
            s1 = slot_ref[2 * j + 1]
            col = lax.broadcasted_iota(jnp.int32, (BLOCK, 2 * BLOCK), 1)
            bias = jnp.where(col < BLOCK, bias_ref[2 * j], bias_ref[2 * j + 1])
            r0, k0 = s0 // slots, lax.rem(s0, slots)
            r1, k1 = s1 // slots, lax.rem(s1, slots)
            for hd in range(heads):
                kc = pl.ds(hd * HEAD_DIM, HEAD_DIM)
                vc = pl.ds(feat + hd * HEAD_DIM, HEAD_DIM)
                keys = jnp.concatenate([recv[r0, k0, :, kc], recv[r1, k1, :, kc]], axis=0)
                vals = jnp.concatenate([recv[r0, k0, :, vc], recv[r1, k1, :, vc]], axis=0)
                s = lax.dot_general(q_ref[rows, kc], keys, nt, preferred_element_type=jnp.float32)
                s = s * scale + bias
                m0 = m_ref[rows, kc]
                m = jnp.maximum(m0, jnp.max(s, axis=1, keepdims=True))
                alpha = jnp.exp(m0 - m)
                p = jnp.exp(s - m)
                tot = l_ref[rows, kc] * alpha + jnp.sum(p, axis=1, keepdims=True)
                o = jnp.dot(p.astype(jnp.bfloat16), vals, preferred_element_type=jnp.float32)
                o = o + acc[rows, kc] * alpha
                att[t, urows, kc] = (o / tot).astype(jnp.bfloat16)
            return c

        lax.fori_loop(0, quarter, one, 0)

    def att_copy(t, g):
        return remote(att.at[t], attr.at[g], att_send.at[t], att_recv.at[g], me, t)

    for t in others:
        far(t)
        att_copy(t, h).start()
    far(h)

    forward(W_CHUNKS - 1)
    w_own.wait()
    ws_copy.wait_recv()
    att_copy(h, sib).wait_recv()

    tile = 512
    tiles = out_ref.shape[1] // tile

    def project_a(i, c):
        cols = pl.ds(pl.multiple_of(i * tile, tile), tile)
        o = jnp.dot(att[h], wall[h, :, cols], preferred_element_type=jnp.float32)
        o = o + jnp.dot(attr[sib], wall[sib, :, cols], preferred_element_type=jnp.float32)
        oacc[:, cols] = o
        return c

    lax.fori_loop(0, tiles, project_a, 0)
    for c in range(W_CHUNKS):
        wf_copy(across_sib, c).wait_recv()
    att_copy(h, across).wait_recv()
    att_copy(h, across_sib).wait_recv()

    def project_b(i, c):
        cols = pl.ds(pl.multiple_of(i * tile, tile), tile)
        o = oacc[:, cols]
        o = o + jnp.dot(attr[across], wall[across, :, cols], preferred_element_type=jnp.float32)
        o = o + jnp.dot(
            attr[across_sib], wall[across_sib, :, cols], preferred_element_type=jnp.float32
        )
        out_ref[:, cols] = o.astype(jnp.bfloat16)
        return c

    lax.fori_loop(0, tiles, project_b, 0)

    def drain(i, c):
        tab_copy(me, peer(i)).wait_send()
        rand_copy(me, peer(i)).wait_send()
        return c

    lax.fori_loop(0, n - 1, drain, 0)

    @pl.when(me == 0)
    def _():
        def go(i, c):
            first_copy(peer(i)).wait_send()
            return c

        lax.fori_loop(0, n - 1, go, 0)

    @pl.when(me == n - 1)
    def _():
        def go(i, c):
            final_copy(peer(i)).wait_send()
            return c

        lax.fori_loop(0, n - 1, go, 0)

    @pl.when(me < n - 1)
    def _():
        to_right().wait_send()

    @pl.when(me > 0)
    def _():
        to_left().wait_send()

    for c in range(W_CHUNKS):
        wx_copy(h, c).wait_send()
        wf_copy(across, c).wait_send()
    ws_copy.wait_send()
    for t in others:
        att_copy(t, h).wait_send()


def body(queries, keys_values, rand_blocks, w_out):
    tok_rows, feat = queries.shape
    heads = feat // HEAD_DIM
    blocks = tok_rows // BLOCK
    n = lax.axis_size("seq")
    n_head = lax.axis_size("head")
    all_blocks = blocks * n
    position = lax.axis_index("seq")
    entries = rand_blocks.shape[0] * rand_blocks.shape[1]
    slots = max(1, entries // n)
    width = w_out.shape[1]

    flat = rand_blocks.reshape(entries)
    owner = flat // blocks
    offset = flat % blocks
    earlier = jnp.arange(entries)[:, None] > jnp.arange(entries)[None, :]
    rank = jnp.sum((owner[:, None] == owner[None, :]) & earlier, axis=1)
    slot = (owner * slots + rank).astype(jnp.int32)
    placed = slot[:, None] == jnp.arange(128)[None, :]
    outgoing = jnp.sum(jnp.where(placed, offset[:, None], 0), axis=0).astype(jnp.int32)
    table = jnp.broadcast_to(outgoing[None, :], (8, 128))

    ids = position * blocks + jnp.arange(blocks, dtype=jnp.int32)
    taken = [ids - 1, ids, ids + 1, jnp.zeros_like(ids), jnp.zeros_like(ids) + (all_blocks - 1)]
    flags = []
    for column in range(rand_blocks.shape[1]):
        chosen = rand_blocks[:, column]
        flags.append(reduce(jnp.logical_or, [chosen == other for other in taken]))
        taken.append(chosen)
    bias = jnp.where(jnp.stack(flags, axis=1), NEG, 0.0).astype(jnp.float32).reshape(entries)

    kv = keys_values.reshape(blocks, BLOCK, 2 * feat)
    vmem = pl.BlockSpec(memory_space=pltpu.VMEM)
    smem = pl.BlockSpec(memory_space=pltpu.SMEM)
    bf16, f32, i32 = jnp.bfloat16, jnp.float32, jnp.int32
    rows_out = tok_rows // n_head
    dma = pltpu.SemaphoreType.DMA
    return pl.pallas_call(
        functools.partial(kernel, n, slots, blocks, heads),
        out_shape=jax.ShapeDtypeStruct((rows_out, width), bf16),
        in_specs=[vmem, vmem, vmem, smem, smem, pl.BlockSpec(memory_space=pl.ANY)],
        out_specs=vmem,
        scratch_shapes=[
            pltpu.VMEM((blocks + 2, BLOCK, 2 * feat), bf16),
            pltpu.VMEM((2, BLOCK, 2 * feat), bf16),
            pltpu.VMEM((n * 8, 128), i32),
            pltpu.SMEM((n * 8, 128), i32),
            pltpu.VMEM((n, slots, BLOCK, 2 * feat), bf16),
            pltpu.VMEM((n, slots, BLOCK, 2 * feat), bf16),
            pltpu.VMEM((tok_rows, feat), f32),
            pltpu.VMEM((tok_rows, feat), f32),
            pltpu.VMEM((tok_rows, feat), f32),
            pltpu.VMEM((n_head, rows_out, feat), bf16),
            pltpu.VMEM((n_head, rows_out, feat), bf16),
            pltpu.VMEM((n_head, feat, width), bf16),
            pltpu.VMEM((rows_out, width), f32),
            dma((n,)),
            dma((n,)),
            dma,
            dma((2,)),
            dma((2,)),
            dma((n,)),
            dma((n,)),
            dma((2,)),
            dma((n,)),
            dma((n,)),
            dma,
            dma((W_CHUNKS,)),
            dma((W_CHUNKS,)),
            dma,
            dma,
            dma((W_CHUNKS,)),
            dma((W_CHUNKS,)),
            dma((n_head,)),
            dma((n_head,)),
        ],
        compiler_params=pltpu.CompilerParams(
            collective_id=0, has_side_effects=True, vmem_limit_bytes=60 * 1024 * 1024
        ),
        cost_estimate=pl.CostEstimate(
            flops=6_000_000_000, bytes_accessed=20_000_000, transcendentals=2_000_000
        ),
    )(queries, kv, table, slot, bias, w_out)


def solution(mesh):
    in_specs = (P("seq", "head"), P("seq", None, "head"), P("seq", None), P("head", None))
    out_specs = P(("seq", "head"), None)
    return jax.shard_map(body, mesh=mesh, in_specs=in_specs, out_specs=out_specs, check_vma=False)
```

```python
import functools
from functools import reduce

import jax
import jax.numpy as jnp
from jax import lax
from jax.experimental import pallas as pl
from jax.experimental.pallas import tpu as pltpu
from jax.sharding import PartitionSpec as P

HEAD_DIM = 128
BLOCK = 64
W_CHUNKS = 4
NEG = -1e30


def kernel(
    n,
    slots,
    blocks,
    heads,
    q_ref,
    kv_ref,
    tab_ref,
    slot_ref,
    bias_ref,
    w_ref,
    out_ref,
    kvp,
    ends,
    tabs,
    tabs_s,
    stage,
    recv_0,
    recv_1,
    recv_2,
    recv_3,
    m_ref,
    l_ref,
    acc,
    att,
    attr,
    wall,
    oacc,
    tab_send,
    tab_recv,
    tab_local,
    halo_send,
    halo_recv,
    first_send,
    final_send,
    ends_recv,
    rand_send,
    rand_recv,
    w_local,
    wx_send,
    wx_recv,
    ws_send,
    ws_recv,
    wf_send,
    wf_recv,
    wy_send,
    wy_recv,
    att_send,
    att_recv,
):
    recvs = (recv_0, recv_1, recv_2, recv_3)
    me = lax.axis_index("seq")
    h = lax.axis_index("head")
    sib = h + 1 - 2 * lax.rem(h, 2)
    across = lax.rem(h + 2, 4)
    across_sib = lax.rem(sib + 2, 4)
    others = (across, across_sib, sib)
    total_blocks = n * blocks
    scale = HEAD_DIM ** (-0.5)
    w_rows = w_ref.shape[0] // W_CHUNKS
    feat = heads * HEAD_DIM

    def remote(src, dst, ssem, rsem, seq, head):
        return pltpu.make_async_remote_copy(
            src_ref=src,
            dst_ref=dst,
            send_sem=ssem,
            recv_sem=rsem,
            device_id=(seq, head),
            device_id_type=pl.DeviceIdType.MESH,
        )

    half = n // 2
    side, place = me // half, lax.rem(me, half)
    pair = me + 1 - 2 * lax.rem(me, 2)

    def peer(i):
        over = 1 - i // half
        k = lax.rem(i, half) + (1 - over)
        return lax.rem(side + over, 2) * half + lax.rem(place + k, half)

    def mate(i):
        return side * half + lax.rem(place + 1 + i, half)

    barrier = pltpu.get_barrier_semaphore()

    def greet(i, c):
        pl.semaphore_signal(
            barrier, inc=1, device_id=(peer(i), h), device_id_type=pl.DeviceIdType.MESH
        )
        return c

    lax.fori_loop(0, n - 1, greet, 0)
    for g in others:
        pl.semaphore_signal(barrier, inc=1, device_id=(me, g), device_id_type=pl.DeviceIdType.MESH)
    pl.semaphore_wait(barrier, n - 1 + 3)

    def tab_copy(s, dest):
        return remote(
            tab_ref, tabs.at[pl.ds(s * 8, 8)], tab_send.at[dest], tab_recv.at[s], dest, h
        )

    def tab_start(i, c):
        tab_copy(me, peer(i)).start()
        return c

    lax.fori_loop(0, n - 1, tab_start, 0)

    def to_right():
        return remote(
            kv_ref.at[blocks - 1], kvp.at[0], halo_send.at[0], halo_recv.at[0], lax.rem(me + 1, n), h
        )

    def to_left():
        return remote(
            kv_ref.at[0],
            kvp.at[blocks + 1],
            halo_send.at[1],
            halo_recv.at[1],
            lax.rem(me + n - 1, n),
            h,
        )

    def first_copy(dest):
        return remote(kv_ref.at[0], ends.at[0], first_send.at[dest], ends_recv.at[0], dest, h)

    def final_copy(dest):
        return remote(kv_ref.at[blocks - 1], ends.at[1], final_send.at[dest], ends_recv.at[1], dest, h)

    def first_relay(dest):
        return remote(ends.at[0], ends.at[0], first_send.at[dest], ends_recv.at[0], dest, h)

    def final_relay(dest):
        return remote(ends.at[1], ends.at[1], final_send.at[dest], ends_recv.at[1], dest, h)

    def to_mates(copy):
        def go(i, c):
            copy(mate(i)).start()
            return c

        lax.fori_loop(0, half - 1, go, 0)

    @pl.when(me == 0)
    def _():
        first_copy(half).start()
        to_mates(first_copy)
        ends[0] = kv_ref[0]
        kvp[0] = jnp.zeros_like(kvp[0])

    @pl.when(me == n - 1)
    def _():
        final_copy(half - 1).start()
        to_mates(final_copy)
        ends[1] = kv_ref[blocks - 1]
        kvp[blocks + 1] = jnp.zeros_like(kvp[0])

    @pl.when(me < n - 1)
    def _():
        to_right().start()

    @pl.when(me > 0)
    def _():
        to_left().start()

    odd = lax.rem(me, 2)

    def w_span(c):
        place_c = c + odd * (W_CHUNKS - 1 - 2 * c)
        return pl.ds(pl.multiple_of(place_c * w_rows, w_rows), w_rows)

    def w_piece(g, c):
        return wall.at[g, w_span(c)]

    def wx_copy(g, c):
        return remote(
            w_ref.at[w_span(c)],
            w_piece(g, c),
            wx_send.at[c],
            wx_recv.at[c],
            me,
            across,
        )

    for c in range(W_CHUNKS - 1):
        wx_copy(h, c).start()

    def tab_wait(i, c):
        tab_copy(peer(i), me).wait_recv()
        return c

    lax.fori_loop(0, n - 1, tab_wait, 0)
    tabs[pl.ds(pl.multiple_of(me * 8, 8), 8), :] = tab_ref[...]
    to_smem = pltpu.make_async_copy(tabs, tabs_s, tab_local)
    to_smem.start()
    to_smem.wait()

    def rand_copy(hd, s, dest):
        return remote(
            stage.at[hd, dest],
            recvs[hd].at[s],
            rand_send.at[hd * n + dest],
            rand_recv.at[hd * n + s],
            dest,
            h,
        )

    def pick(buf, hd, dest):
        for k in range(slots):
            block = tabs_s[dest * 8, me * slots + k]
            buf[k, :, :HEAD_DIM] = kv_ref[block, :, pl.ds(hd * HEAD_DIM, HEAD_DIM)]
            buf[k, :, HEAD_DIM:] = kv_ref[block, :, pl.ds(feat + hd * HEAD_DIM, HEAD_DIM)]

    for hd in range(heads):

        def rand_start(i, c, hd=hd):
            dest = peer(i)
            pick(stage.at[hd, dest], hd, dest)
            rand_copy(hd, me, dest).start()
            return c

        lax.fori_loop(0, n - 1, rand_start, 0)
    for hd in range(heads):
        pick(recvs[hd].at[me], hd, me)

    w_own = pltpu.make_async_copy(w_ref, wall.at[h], w_local)
    w_own.start()
    ws_copy = remote(w_ref, wall.at[h], ws_send, ws_recv, me, sib)
    ws_copy.start()

    def fill(j, c):
        kvp[j + 1] = kv_ref[j]
        return c

    lax.fori_loop(0, blocks, fill, 0)

    @pl.when(me > 0)
    def _():
        to_right().wait_recv()
        first_copy(me).wait_recv()

        @pl.when(me == half)
        def _():
            to_mates(first_relay)

    @pl.when(me < n - 1)
    def _():
        to_left().wait_recv()
        final_copy(me).wait_recv()

        @pl.when(me == half - 1)
        def _():
            to_mates(final_relay)

    nt = (((1,), (1,)), ((), ()))

    def near(j, c):
        block = me * blocks + j
        rows = pl.ds(pl.multiple_of(j * BLOCK, BLOCK), BLOCK)
        b_prev = jnp.where(block >= 1, 0.0, NEG)
        b_next = jnp.where(block <= total_blocks - 2, 0.0, NEG)
        b_first = jnp.where(block >= 2, 0.0, NEG)
        b_final = jnp.where(block <= total_blocks - 3, 0.0, NEG)
        col = lax.broadcasted_iota(jnp.int32, (BLOCK, 3 * BLOCK), 1)
        b_win = jnp.where(col < BLOCK, b_prev, jnp.where(col >= 2 * BLOCK, b_next, 0.0))
        cole = lax.broadcasted_iota(jnp.int32, (BLOCK, 2 * BLOCK), 1)
        b_end = jnp.where(cole < BLOCK, b_first, b_final)
        for hd in range(heads):
            kc = pl.ds(hd * HEAD_DIM, HEAD_DIM)
            vc = pl.ds(feat + hd * HEAD_DIM, HEAD_DIM)
            qh = q_ref[rows, kc]
            kw = kvp[pl.ds(j, 3), :, kc].reshape(3 * BLOCK, HEAD_DIM)
            vw = kvp[pl.ds(j, 3), :, vc].reshape(3 * BLOCK, HEAD_DIM)
            ke = ends[:, :, kc].reshape(2 * BLOCK, HEAD_DIM)
            ve = ends[:, :, vc].reshape(2 * BLOCK, HEAD_DIM)
            sw = lax.dot_general(qh, kw, nt, preferred_element_type=jnp.float32) * scale + b_win
            se = lax.dot_general(qh, ke, nt, preferred_element_type=jnp.float32) * scale + b_end
            m = jnp.maximum(
                jnp.max(sw, axis=1, keepdims=True), jnp.max(se, axis=1, keepdims=True)
            )
            pw = jnp.exp(sw - m)
            pe = jnp.exp(se - m)
            tot = jnp.sum(pw, axis=1, keepdims=True) + jnp.sum(pe, axis=1, keepdims=True)
            o = jnp.dot(pw.astype(jnp.bfloat16), vw, preferred_element_type=jnp.float32)
            o = o + jnp.dot(pe.astype(jnp.bfloat16), ve, preferred_element_type=jnp.float32)
            m_ref[rows, kc] = jnp.broadcast_to(m, (BLOCK, HEAD_DIM))
            l_ref[rows, kc] = jnp.broadcast_to(tot, (BLOCK, HEAD_DIM))
            acc[rows, kc] = o
        return c

    lax.fori_loop(0, blocks, near, 0)

    def wf_copy(g, c):
        return remote(w_piece(g, c), w_piece(g, c), wf_send.at[c], wf_recv.at[c], me, sib)

    def wy_copy(span):
        return remote(wall.at[across, span], wall.at[across, span], wy_send, wy_recv, pair, h)

    last = W_CHUNKS - 1

    def rand_wait(hd):
        def go(i, c):
            rand_copy(hd, peer(i), me).wait_recv()
            return c

        lax.fori_loop(0, n - 1, go, 0)

    quarter = blocks // 4

    def att_copy(hd, t, g):
        return remote(
            att.at[hd, t], attr.at[hd, g], att_send.at[hd * 4 + t], att_recv.at[hd * 4 + g], me, t
        )

    def far(hd):
        kc = pl.ds(hd * HEAD_DIM, HEAD_DIM)

        def one(i, c):
            t = 2 * lax.rem(h // 2 + 1 + i // 2, 2) + lax.rem(h + i, 2)
            for u in range(quarter):
                j = t * quarter + u
                rows = pl.ds(pl.multiple_of(j * BLOCK, BLOCK), BLOCK)
                s0 = slot_ref[2 * j]
                s1 = slot_ref[2 * j + 1]
                col = lax.broadcasted_iota(jnp.int32, (BLOCK, 2 * BLOCK), 1)
                bias = jnp.where(col < BLOCK, bias_ref[2 * j], bias_ref[2 * j + 1])
                r0, k0 = s0 // slots, lax.rem(s0, slots)
                r1, k1 = s1 // slots, lax.rem(s1, slots)
                both = jnp.concatenate([recvs[hd][r0, k0], recvs[hd][r1, k1]], axis=0)
                keys, vals = both[:, :HEAD_DIM], both[:, HEAD_DIM:]
                s = lax.dot_general(q_ref[rows, kc], keys, nt, preferred_element_type=jnp.float32)
                s = s * scale + bias
                m0 = m_ref[rows, kc]
                m = jnp.maximum(m0, jnp.max(s, axis=1, keepdims=True))
                alpha = jnp.exp(m0 - m)
                p = jnp.exp(s - m)
                tot = l_ref[rows, kc] * alpha + jnp.sum(p, axis=1, keepdims=True)
                o = jnp.dot(p.astype(jnp.bfloat16), vals, preferred_element_type=jnp.float32)
                o = o + acc[rows, kc] * alpha
                att[hd, t, u * BLOCK : (u + 1) * BLOCK, :] = (o / tot).astype(jnp.bfloat16)

            @pl.when(i != 2)
            def _():
                att_copy(hd, t, h).start()

            return c

        lax.fori_loop(0, 4, one, 0)

    for hd in range(heads):
        if hd < last:
            wx_copy(across, hd).wait_recv()
            wf_copy(across, hd).start()
        if hd == 0:
            wy_copy(w_span(0)).start()
        if hd == last:
            wy_copy(w_span(last)).wait_recv()
            wf_copy(across, last).start()
        rand_wait(hd)
        far(hd)

    w_own.wait()
    ws_copy.wait_recv()
    for c in range(W_CHUNKS):
        wf_copy(across_sib, c).wait_recv()
    for hd in range(heads):
        att_copy(hd, h, sib).wait_recv()
    for hd in range(heads - 1):
        att_copy(hd, h, across).wait_recv()
        att_copy(hd, h, across_sib).wait_recv()

    tile = 512
    tiles = out_ref.shape[1] // tile
    early = (heads - 1) * HEAD_DIM

    def joined(buf, g, count):
        return jnp.concatenate([buf[hd, g] for hd in range(count)], axis=1)

    def project_a(i, c):
        cols = pl.ds(pl.multiple_of(i * tile, tile), tile)
        o = jnp.dot(joined(att, h, heads), wall[h, :, cols], preferred_element_type=jnp.float32)
        for g, buf, count in (
            (sib, attr, heads),
            (across, attr, heads - 1),
            (across_sib, attr, heads - 1),
        ):
            o = o + jnp.dot(
                joined(buf, g, count),
                wall[g, : count * HEAD_DIM, cols],
                preferred_element_type=jnp.float32,
            )
        oacc[:, cols] = o
        return c

    lax.fori_loop(0, tiles, project_a, 0)
    att_copy(heads - 1, h, across).wait_recv()
    att_copy(heads - 1, h, across_sib).wait_recv()

    def project_b(i, c):
        cols = pl.ds(pl.multiple_of(i * tile, tile), tile)
        o = oacc[:, cols]
        for g in (across, across_sib):
            o = o + jnp.dot(
                attr[heads - 1, g], wall[g, early:, cols], preferred_element_type=jnp.float32
            )
        out_ref[:, cols] = o.astype(jnp.bfloat16)
        return c

    lax.fori_loop(0, tiles, project_b, 0)

    def drain(i, c):
        tab_copy(me, peer(i)).wait_send()
        for hd in range(heads):
            rand_copy(hd, me, peer(i)).wait_send()
        return c

    lax.fori_loop(0, n - 1, drain, 0)

    def from_mates(copy):
        def go(i, c):
            copy(mate(i)).wait_send()
            return c

        lax.fori_loop(0, half - 1, go, 0)

    @pl.when(me == 0)
    def _():
        first_copy(half).wait_send()
        from_mates(first_copy)

    @pl.when(me == n - 1)
    def _():
        final_copy(half - 1).wait_send()
        from_mates(final_copy)

    @pl.when(me == half)
    def _():
        from_mates(first_relay)

    @pl.when(me == half - 1)
    def _():
        from_mates(final_relay)

    @pl.when(me < n - 1)
    def _():
        to_right().wait_send()

    @pl.when(me > 0)
    def _():
        to_left().wait_send()

    for c in range(W_CHUNKS):
        if c < last:
            wx_copy(h, c).wait_send()
        wf_copy(across, c).wait_send()
    wy_copy(w_span(0)).wait_send()
    ws_copy.wait_send()
    for hd in range(heads):
        for t in others:
            att_copy(hd, t, h).wait_send()


def body(queries, keys_values, rand_blocks, w_out):
    tok_rows, feat = queries.shape
    heads = feat // HEAD_DIM
    blocks = tok_rows // BLOCK
    n = lax.axis_size("seq")
    n_head = lax.axis_size("head")
    all_blocks = blocks * n
    position = lax.axis_index("seq")
    entries = rand_blocks.shape[0] * rand_blocks.shape[1]
    slots = max(1, entries // n)
    width = w_out.shape[1]

    flat = rand_blocks.reshape(entries)
    owner = flat // blocks
    offset = flat % blocks
    earlier = jnp.arange(entries)[:, None] > jnp.arange(entries)[None, :]
    rank = jnp.sum((owner[:, None] == owner[None, :]) & earlier, axis=1)
    slot = (owner * slots + rank).astype(jnp.int32)
    placed = slot[:, None] == jnp.arange(128)[None, :]
    outgoing = jnp.sum(jnp.where(placed, offset[:, None], 0), axis=0).astype(jnp.int32)
    table = jnp.broadcast_to(outgoing[None, :], (8, 128))

    ids = position * blocks + jnp.arange(blocks, dtype=jnp.int32)
    taken = [ids - 1, ids, ids + 1, jnp.zeros_like(ids), jnp.zeros_like(ids) + (all_blocks - 1)]
    flags = []
    for column in range(rand_blocks.shape[1]):
        chosen = rand_blocks[:, column]
        flags.append(reduce(jnp.logical_or, [chosen == other for other in taken]))
        taken.append(chosen)
    bias = jnp.where(jnp.stack(flags, axis=1), NEG, 0.0).astype(jnp.float32).reshape(entries)

    kv = keys_values.reshape(blocks, BLOCK, 2 * feat)
    vmem = pl.BlockSpec(memory_space=pltpu.VMEM)
    smem = pl.BlockSpec(memory_space=pltpu.SMEM)
    bf16, f32, i32 = jnp.bfloat16, jnp.float32, jnp.int32
    rows_out = tok_rows // n_head
    dma = pltpu.SemaphoreType.DMA
    return pl.pallas_call(
        functools.partial(kernel, n, slots, blocks, heads),
        out_shape=jax.ShapeDtypeStruct((rows_out, width), bf16),
        in_specs=[vmem, vmem, vmem, smem, smem, pl.BlockSpec(memory_space=pl.ANY)],
        out_specs=vmem,
        scratch_shapes=[
            pltpu.VMEM((blocks + 2, BLOCK, 2 * feat), bf16),
            pltpu.VMEM((2, BLOCK, 2 * feat), bf16),
            pltpu.VMEM((n * 8, 128), i32),
            pltpu.SMEM((n * 8, 128), i32),
            pltpu.VMEM((heads, n, slots, BLOCK, 2 * HEAD_DIM), bf16),
            *[pltpu.VMEM((n, slots, BLOCK, 2 * HEAD_DIM), bf16)] * 4,
            pltpu.VMEM((tok_rows, feat), f32),
            pltpu.VMEM((tok_rows, feat), f32),
            pltpu.VMEM((tok_rows, feat), f32),
            pltpu.VMEM((heads, n_head, rows_out, HEAD_DIM), bf16),
            pltpu.VMEM((heads, n_head, rows_out, HEAD_DIM), bf16),
            pltpu.VMEM((n_head, feat, width), bf16),
            pltpu.VMEM((rows_out, width), f32),
            dma((n,)),
            dma((n,)),
            dma,
            dma((2,)),
            dma((2,)),
            dma((n,)),
            dma((n,)),
            dma((2,)),
            dma((heads * n,)),
            dma((heads * n,)),
            dma,
            dma((W_CHUNKS,)),
            dma((W_CHUNKS,)),
            dma,
            dma,
            dma((W_CHUNKS,)),
            dma((W_CHUNKS,)),
            dma,
            dma,
            dma((heads * n_head,)),
            dma((heads * n_head,)),
        ],
        compiler_params=pltpu.CompilerParams(
            collective_id=0, has_side_effects=True, vmem_limit_bytes=60 * 1024 * 1024
        ),
        cost_estimate=pl.CostEstimate(
            flops=6_000_000_000, bytes_accessed=20_000_000, transcendentals=2_000_000
        ),
    )(queries, kv, table, slot, bias, w_out)


def solution(mesh):
    in_specs = (P("seq", "head"), P("seq", None, "head"), P("seq", None), P("head", None))
    out_specs = P(("seq", "head"), None)
    return jax.shard_map(body, mesh=mesh, in_specs=in_specs, out_specs=out_specs, check_vma=False)
```

```python
import functools
from functools import reduce

import jax
import jax.numpy as jnp
from jax import lax
from jax.experimental import pallas as pl
from jax.experimental.pallas import tpu as pltpu
from jax.sharding import PartitionSpec as P

HEAD_DIM = 128
BLOCK = 64
W_CHUNKS = 4
NEG = -1e30


def kernel(
    n,
    slots,
    blocks,
    heads,
    q_ref,
    kv_ref,
    tab_ref,
    slot_ref,
    bias_ref,
    w_ref,
    out_ref,
    kvp,
    ends,
    tabs,
    tabs_s,
    stage,
    recv_0,
    recv_1,
    recv_2,
    recv_3,
    m_ref,
    l_ref,
    acc,
    att,
    attr,
    wall,
    oacc,
    tab_send,
    tab_recv,
    tab_local,
    halo_send,
    halo_recv,
    first_send,
    final_send,
    ends_recv,
    rand_send,
    rand_recv,
    w_local,
    wx_send,
    wx_recv,
    ws_send,
    ws_recv,
    wf_send,
    wf_recv,
    wy_send,
    wy_recv,
    att_send,
    att_recv,
):
    recvs = (recv_0, recv_1, recv_2, recv_3)
    me = lax.axis_index("seq")
    h = lax.axis_index("head")
    sib = h + 1 - 2 * lax.rem(h, 2)
    across = lax.rem(h + 2, 4)
    across_sib = lax.rem(sib + 2, 4)
    others = (across, across_sib, sib)
    total_blocks = n * blocks
    scale = HEAD_DIM ** (-0.5)
    w_rows = w_ref.shape[0] // W_CHUNKS
    feat = heads * HEAD_DIM

    def remote(src, dst, ssem, rsem, seq, head):
        return pltpu.make_async_remote_copy(
            src_ref=src,
            dst_ref=dst,
            send_sem=ssem,
            recv_sem=rsem,
            device_id=(seq, head),
            device_id_type=pl.DeviceIdType.MESH,
        )

    half = n // 2
    side, place = me // half, lax.rem(me, half)
    pair = me + 1 - 2 * lax.rem(me, 2)

    deep = half // 2
    level, lane = place // 2, lax.rem(place, 2)
    inner = lax.rem(level + side + 1, 2)

    def peer(i):
        i = lax.rem(i + inner + n - 2, n - 1)
        over = 1 - lax.rem(i, 2)
        k = (i + 1) // 2
        to_level = lax.rem(level + lax.rem(k, deep), deep)
        to_lane = lax.rem(lane + k // deep, 2)
        return lax.rem(side + over, 2) * half + to_level * 2 + to_lane

    def mate(i):
        return side * half + lax.rem(place + 1 + i, half)

    barrier = pltpu.get_barrier_semaphore()

    def greet(i, c):
        pl.semaphore_signal(
            barrier, inc=1, device_id=(peer(i), h), device_id_type=pl.DeviceIdType.MESH
        )
        return c

    lax.fori_loop(0, n - 1, greet, 0)
    for g in others:
        pl.semaphore_signal(barrier, inc=1, device_id=(me, g), device_id_type=pl.DeviceIdType.MESH)
    pl.semaphore_wait(barrier, n - 1 + 3)

    def tab_copy(s, dest):
        return remote(
            tab_ref, tabs.at[pl.ds(s * 8, 8)], tab_send.at[dest], tab_recv.at[s], dest, h
        )

    def tab_start(i, c):
        tab_copy(me, peer(i)).start()
        return c

    lax.fori_loop(0, n - 1, tab_start, 0)

    def to_right():
        return remote(
            kv_ref.at[blocks - 1], kvp.at[0], halo_send.at[0], halo_recv.at[0], lax.rem(me + 1, n), h
        )

    def to_left():
        return remote(
            kv_ref.at[0],
            kvp.at[blocks + 1],
            halo_send.at[1],
            halo_recv.at[1],
            lax.rem(me + n - 1, n),
            h,
        )

    def first_copy(dest):
        return remote(kv_ref.at[0], ends.at[0], first_send.at[dest], ends_recv.at[0], dest, h)

    def final_copy(dest):
        return remote(kv_ref.at[blocks - 1], ends.at[1], final_send.at[dest], ends_recv.at[1], dest, h)

    def first_relay(dest):
        return remote(ends.at[0], ends.at[0], first_send.at[dest], ends_recv.at[0], dest, h)

    def final_relay(dest):
        return remote(ends.at[1], ends.at[1], final_send.at[dest], ends_recv.at[1], dest, h)

    def to_mates(copy):
        def go(i, c):
            copy(mate(i)).start()
            return c

        lax.fori_loop(0, half - 1, go, 0)

    @pl.when(me == 0)
    def _():
        first_copy(half).start()
        to_mates(first_copy)
        ends[0] = kv_ref[0]
        kvp[0] = jnp.zeros_like(kvp[0])

    @pl.when(me == n - 1)
    def _():
        final_copy(half - 1).start()
        to_mates(final_copy)
        ends[1] = kv_ref[blocks - 1]
        kvp[blocks + 1] = jnp.zeros_like(kvp[0])

    @pl.when(me < n - 1)
    def _():
        to_right().start()

    @pl.when(me > 0)
    def _():
        to_left().start()

    odd = lax.rem(me, 2)

    def w_span(c):
        place_c = c + odd * (W_CHUNKS - 1 - 2 * c)
        return pl.ds(pl.multiple_of(place_c * w_rows, w_rows), w_rows)

    def w_piece(g, c):
        return wall.at[g, w_span(c)]

    def wx_copy(g, c):
        return remote(
            w_ref.at[w_span(c)],
            w_piece(g, c),
            wx_send.at[c],
            wx_recv.at[c],
            me,
            across,
        )

    for c in range(W_CHUNKS - 1):
        wx_copy(h, c).start()

    def tab_wait(i, c):
        tab_copy(peer(i), me).wait_recv()
        return c

    lax.fori_loop(0, n - 1, tab_wait, 0)
    tabs[pl.ds(pl.multiple_of(me * 8, 8), 8), :] = tab_ref[...]
    to_smem = pltpu.make_async_copy(tabs, tabs_s, tab_local)
    to_smem.start()
    to_smem.wait()

    def rand_copy(hd, s, dest):
        return remote(
            stage.at[hd, dest],
            recvs[hd].at[s],
            rand_send.at[hd * n + dest],
            rand_recv.at[hd * n + s],
            dest,
            h,
        )

    def pick(buf, hd, dest):
        for k in range(slots):
            block = tabs_s[dest * 8, me * slots + k]
            buf[k, :, :HEAD_DIM] = kv_ref[block, :, pl.ds(hd * HEAD_DIM, HEAD_DIM)]
            buf[k, :, HEAD_DIM:] = kv_ref[block, :, pl.ds(feat + hd * HEAD_DIM, HEAD_DIM)]

    for hd in range(heads):

        def rand_start(i, c, hd=hd):
            dest = peer(i)
            pick(stage.at[hd, dest], hd, dest)
            rand_copy(hd, me, dest).start()
            return c

        lax.fori_loop(0, n - 1, rand_start, 0)
    for hd in range(heads):
        pick(recvs[hd].at[me], hd, me)

    w_own = pltpu.make_async_copy(w_ref, wall.at[h], w_local)
    w_own.start()
    ws_copy = remote(w_ref, wall.at[h], ws_send, ws_recv, me, sib)
    ws_copy.start()

    def fill(j, c):
        kvp[j + 1] = kv_ref[j]
        return c

    lax.fori_loop(0, blocks, fill, 0)

    @pl.when(me > 0)
    def _():
        to_right().wait_recv()
        first_copy(me).wait_recv()

        @pl.when(me == half)
        def _():
            to_mates(first_relay)

    @pl.when(me < n - 1)
    def _():
        to_left().wait_recv()
        final_copy(me).wait_recv()

        @pl.when(me == half - 1)
        def _():
            to_mates(final_relay)

    nt = (((1,), (1,)), ((), ()))

    def near(j, c):
        block = me * blocks + j
        rows = pl.ds(pl.multiple_of(j * BLOCK, BLOCK), BLOCK)
        b_prev = jnp.where(block >= 1, 0.0, NEG)
        b_next = jnp.where(block <= total_blocks - 2, 0.0, NEG)
        b_first = jnp.where(block >= 2, 0.0, NEG)
        b_final = jnp.where(block <= total_blocks - 3, 0.0, NEG)
        col = lax.broadcasted_iota(jnp.int32, (BLOCK, 3 * BLOCK), 1)
        b_win = jnp.where(col < BLOCK, b_prev, jnp.where(col >= 2 * BLOCK, b_next, 0.0))
        cole = lax.broadcasted_iota(jnp.int32, (BLOCK, 2 * BLOCK), 1)
        b_end = jnp.where(cole < BLOCK, b_first, b_final)
        for hd in range(heads):
            kc = pl.ds(hd * HEAD_DIM, HEAD_DIM)
            vc = pl.ds(feat + hd * HEAD_DIM, HEAD_DIM)
            qh = q_ref[rows, kc]
            kw = kvp[pl.ds(j, 3), :, kc].reshape(3 * BLOCK, HEAD_DIM)
            vw = kvp[pl.ds(j, 3), :, vc].reshape(3 * BLOCK, HEAD_DIM)
            ke = ends[:, :, kc].reshape(2 * BLOCK, HEAD_DIM)
            ve = ends[:, :, vc].reshape(2 * BLOCK, HEAD_DIM)
            sw = lax.dot_general(qh, kw, nt, preferred_element_type=jnp.float32) * scale + b_win
            se = lax.dot_general(qh, ke, nt, preferred_element_type=jnp.float32) * scale + b_end
            m = jnp.maximum(
                jnp.max(sw, axis=1, keepdims=True), jnp.max(se, axis=1, keepdims=True)
            )
            pw = jnp.exp(sw - m)
            pe = jnp.exp(se - m)
            tot = jnp.sum(pw, axis=1, keepdims=True) + jnp.sum(pe, axis=1, keepdims=True)
            o = jnp.dot(pw.astype(jnp.bfloat16), vw, preferred_element_type=jnp.float32)
            o = o + jnp.dot(pe.astype(jnp.bfloat16), ve, preferred_element_type=jnp.float32)
            m_ref[rows, kc] = jnp.broadcast_to(m, (BLOCK, HEAD_DIM))
            l_ref[rows, kc] = jnp.broadcast_to(tot, (BLOCK, HEAD_DIM))
            acc[rows, kc] = o
        return c

    lax.fori_loop(0, blocks, near, 0)

    def wf_copy(g, c):
        return remote(w_piece(g, c), w_piece(g, c), wf_send.at[c], wf_recv.at[c], me, sib)

    def wy_copy(span):
        return remote(wall.at[across, span], wall.at[across, span], wy_send, wy_recv, pair, h)

    last = W_CHUNKS - 1

    def rand_wait(hd):
        def go(i, c):
            rand_copy(hd, peer(i), me).wait_recv()
            return c

        lax.fori_loop(0, n - 1, go, 0)

    quarter = blocks // 4

    def att_copy(hd, t, g):
        return remote(
            att.at[hd, t], attr.at[hd, g], att_send.at[hd * 4 + t], att_recv.at[hd * 4 + g], me, t
        )

    def far(hd):
        kc = pl.ds(hd * HEAD_DIM, HEAD_DIM)

        def one(i, c):
            t = 2 * lax.rem(h // 2 + 1 + i // 2, 2) + lax.rem(h + i, 2)
            for u in range(quarter):
                j = t * quarter + u
                rows = pl.ds(pl.multiple_of(j * BLOCK, BLOCK), BLOCK)
                s0 = slot_ref[2 * j]
                s1 = slot_ref[2 * j + 1]
                col = lax.broadcasted_iota(jnp.int32, (BLOCK, 2 * BLOCK), 1)
                bias = jnp.where(col < BLOCK, bias_ref[2 * j], bias_ref[2 * j + 1])
                r0, k0 = s0 // slots, lax.rem(s0, slots)
                r1, k1 = s1 // slots, lax.rem(s1, slots)
                both = jnp.concatenate([recvs[hd][r0, k0], recvs[hd][r1, k1]], axis=0)
                keys, vals = both[:, :HEAD_DIM], both[:, HEAD_DIM:]
                s = lax.dot_general(q_ref[rows, kc], keys, nt, preferred_element_type=jnp.float32)
                s = s * scale + bias
                m0 = m_ref[rows, kc]
                m = jnp.maximum(m0, jnp.max(s, axis=1, keepdims=True))
                alpha = jnp.exp(m0 - m)
                p = jnp.exp(s - m)
                tot = l_ref[rows, kc] * alpha + jnp.sum(p, axis=1, keepdims=True)
                o = jnp.dot(p.astype(jnp.bfloat16), vals, preferred_element_type=jnp.float32)
                o = o + acc[rows, kc] * alpha
                att[hd, t, u * BLOCK : (u + 1) * BLOCK, :] = (o / tot).astype(jnp.bfloat16)

            @pl.when(i != 2)
            def _():
                att_copy(hd, t, h).start()

            return c

        lax.fori_loop(0, 4, one, 0)

    tile = 512
    tiles = out_ref.shape[1] // tile
    early = (heads - 1) * HEAD_DIM

    def joined(buf, g):
        return jnp.concatenate([buf[hd, g] for hd in range(heads - 1)], axis=1)

    def project_a(i, c):
        cols = pl.ds(pl.multiple_of(i * tile, tile), tile)
        o = jnp.dot(joined(att, h), wall[h, :early, cols], preferred_element_type=jnp.float32)
        for g in (sib, across, across_sib):
            o = o + jnp.dot(
                joined(attr, g), wall[g, :early, cols], preferred_element_type=jnp.float32
            )
        oacc[:, cols] = o
        return c

    def project_b(i, c):
        cols = pl.ds(pl.multiple_of(i * tile, tile), tile)
        o = oacc[:, cols]
        o = o + jnp.dot(att[last, h], wall[h, early:, cols], preferred_element_type=jnp.float32)
        for g in (sib, across, across_sib):
            o = o + jnp.dot(
                attr[last, g], wall[g, early:, cols], preferred_element_type=jnp.float32
            )
        out_ref[:, cols] = o.astype(jnp.bfloat16)
        return c

    for hd in range(heads):
        if hd < last:
            wx_copy(across, hd).wait_recv()
            wf_copy(across, hd).start()
        if hd == 0:
            wy_copy(w_span(0)).start()
        if hd == last:
            wy_copy(w_span(last)).wait_recv()
            wf_copy(across, last).start()
            w_own.wait()
            ws_copy.wait_recv()
            for c in range(W_CHUNKS):
                wf_copy(across_sib, c).wait_recv()
            for e in range(last):
                for g in others:
                    att_copy(e, h, g).wait_recv()
            lax.fori_loop(0, tiles, project_a, 0)
        rand_wait(hd)
        far(hd)

    for g in others:
        att_copy(last, h, g).wait_recv()
    lax.fori_loop(0, tiles, project_b, 0)

    def drain(i, c):
        tab_copy(me, peer(i)).wait_send()
        for hd in range(heads):
            rand_copy(hd, me, peer(i)).wait_send()
        return c

    lax.fori_loop(0, n - 1, drain, 0)

    def from_mates(copy):
        def go(i, c):
            copy(mate(i)).wait_send()
            return c

        lax.fori_loop(0, half - 1, go, 0)

    @pl.when(me == 0)
    def _():
        first_copy(half).wait_send()
        from_mates(first_copy)

    @pl.when(me == n - 1)
    def _():
        final_copy(half - 1).wait_send()
        from_mates(final_copy)

    @pl.when(me == half)
    def _():
        from_mates(first_relay)

    @pl.when(me == half - 1)
    def _():
        from_mates(final_relay)

    @pl.when(me < n - 1)
    def _():
        to_right().wait_send()

    @pl.when(me > 0)
    def _():
        to_left().wait_send()

    for c in range(W_CHUNKS):
        if c < last:
            wx_copy(h, c).wait_send()
        wf_copy(across, c).wait_send()
    wy_copy(w_span(0)).wait_send()
    ws_copy.wait_send()
    for hd in range(heads):
        for t in others:
            att_copy(hd, t, h).wait_send()


def body(queries, keys_values, rand_blocks, w_out):
    tok_rows, feat = queries.shape
    heads = feat // HEAD_DIM
    blocks = tok_rows // BLOCK
    n = lax.axis_size("seq")
    n_head = lax.axis_size("head")
    all_blocks = blocks * n
    position = lax.axis_index("seq")
    entries = rand_blocks.shape[0] * rand_blocks.shape[1]
    slots = max(1, entries // n)
    width = w_out.shape[1]

    flat = rand_blocks.reshape(entries)
    owner = flat // blocks
    offset = flat % blocks
    earlier = jnp.arange(entries)[:, None] > jnp.arange(entries)[None, :]
    rank = jnp.sum((owner[:, None] == owner[None, :]) & earlier, axis=1)
    slot = (owner * slots + rank).astype(jnp.int32)
    placed = slot[:, None] == jnp.arange(128)[None, :]
    outgoing = jnp.sum(jnp.where(placed, offset[:, None], 0), axis=0).astype(jnp.int32)
    table = jnp.broadcast_to(outgoing[None, :], (8, 128))

    ids = position * blocks + jnp.arange(blocks, dtype=jnp.int32)
    taken = [ids - 1, ids, ids + 1, jnp.zeros_like(ids), jnp.zeros_like(ids) + (all_blocks - 1)]
    flags = []
    for column in range(rand_blocks.shape[1]):
        chosen = rand_blocks[:, column]
        flags.append(reduce(jnp.logical_or, [chosen == other for other in taken]))
        taken.append(chosen)
    bias = jnp.where(jnp.stack(flags, axis=1), NEG, 0.0).astype(jnp.float32).reshape(entries)

    kv = keys_values.reshape(blocks, BLOCK, 2 * feat)
    vmem = pl.BlockSpec(memory_space=pltpu.VMEM)
    smem = pl.BlockSpec(memory_space=pltpu.SMEM)
    bf16, f32, i32 = jnp.bfloat16, jnp.float32, jnp.int32
    rows_out = tok_rows // n_head
    dma = pltpu.SemaphoreType.DMA
    return pl.pallas_call(
        functools.partial(kernel, n, slots, blocks, heads),
        out_shape=jax.ShapeDtypeStruct((rows_out, width), bf16),
        in_specs=[vmem, vmem, vmem, smem, smem, pl.BlockSpec(memory_space=pl.ANY)],
        out_specs=vmem,
        scratch_shapes=[
            pltpu.VMEM((blocks + 2, BLOCK, 2 * feat), bf16),
            pltpu.VMEM((2, BLOCK, 2 * feat), bf16),
            pltpu.VMEM((n * 8, 128), i32),
            pltpu.SMEM((n * 8, 128), i32),
            pltpu.VMEM((heads, n, slots, BLOCK, 2 * HEAD_DIM), bf16),
            *[pltpu.VMEM((n, slots, BLOCK, 2 * HEAD_DIM), bf16)] * 4,
            pltpu.VMEM((tok_rows, feat), f32),
            pltpu.VMEM((tok_rows, feat), f32),
            pltpu.VMEM((tok_rows, feat), f32),
            pltpu.VMEM((heads, n_head, rows_out, HEAD_DIM), bf16),
            pltpu.VMEM((heads, n_head, rows_out, HEAD_DIM), bf16),
            pltpu.VMEM((n_head, feat, width), bf16),
            pltpu.VMEM((rows_out, width), f32),
            dma((n,)),
            dma((n,)),
            dma,
            dma((2,)),
            dma((2,)),
            dma((n,)),
            dma((n,)),
            dma((2,)),
            dma((heads * n,)),
            dma((heads * n,)),
            dma,
            dma((W_CHUNKS,)),
            dma((W_CHUNKS,)),
            dma,
            dma,
            dma((W_CHUNKS,)),
            dma((W_CHUNKS,)),
            dma,
            dma,
            dma((heads * n_head,)),
            dma((heads * n_head,)),
        ],
        compiler_params=pltpu.CompilerParams(
            collective_id=0, has_side_effects=True, vmem_limit_bytes=60 * 1024 * 1024
        ),
        cost_estimate=pl.CostEstimate(
            flops=6_000_000_000, bytes_accessed=20_000_000, transcendentals=2_000_000
        ),
    )(queries, kv, table, slot, bias, w_out)


def solution(mesh):
    in_specs = (P("seq", "head"), P("seq", None, "head"), P("seq", None), P("head", None))
    out_specs = P(("seq", "head"), None)
    return jax.shard_map(body, mesh=mesh, in_specs=in_specs, out_specs=out_specs, check_vma=False)
```

```python
import functools
from functools import reduce

import jax
import jax.numpy as jnp
from jax import lax
from jax.experimental import pallas as pl
from jax.experimental.pallas import tpu as pltpu
from jax.sharding import PartitionSpec as P

HEAD_DIM = 128
BLOCK = 64
W_CHUNKS = 4
NEG = -1e30


def kernel(
    n,
    slots,
    blocks,
    heads,
    q_ref,
    kv_ref,
    tab_ref,
    slot_ref,
    bias_ref,
    w_ref,
    out_ref,
    kvp,
    ends,
    tabs,
    tabs_s,
    stage,
    recv_0,
    recv_1,
    recv_2,
    recv_3,
    m_ref,
    l_ref,
    acc,
    att,
    attr,
    wall,
    oacc,
    tab_send,
    tab_recv,
    tab_local,
    halo_send,
    halo_recv,
    first_send,
    final_send,
    ends_recv,
    rand_send,
    rand_recv,
    w_local,
    wx_send,
    wx_recv,
    ws_send,
    ws_recv,
    wf_send,
    wf_recv,
    wy_send,
    wy_recv,
    att_send,
    att_recv,
):
    recvs = (recv_0, recv_1, recv_2, recv_3)
    me = lax.axis_index("seq")
    h = lax.axis_index("head")
    sib = h + 1 - 2 * lax.rem(h, 2)
    across = lax.rem(h + 2, 4)
    across_sib = lax.rem(sib + 2, 4)
    others = (across, across_sib, sib)
    total_blocks = n * blocks
    scale = HEAD_DIM ** (-0.5)
    w_rows = w_ref.shape[0] // W_CHUNKS
    feat = heads * HEAD_DIM

    def remote(src, dst, ssem, rsem, seq, head):
        return pltpu.make_async_remote_copy(
            src_ref=src,
            dst_ref=dst,
            send_sem=ssem,
            recv_sem=rsem,
            device_id=(seq, head),
            device_id_type=pl.DeviceIdType.MESH,
        )

    half = n // 2
    side, place = me // half, lax.rem(me, half)
    pair = me + 1 - 2 * lax.rem(me, 2)

    deep = half // 2
    level, lane = place // 2, lax.rem(place, 2)

    def peer(i):
        over = 1 - lax.rem(i, 2)
        k = (i + 1) // 2
        inward = lax.rem(k, deep)
        facing = inward + (1 - side) * (deep - 1 - 2 * inward)
        to_level = over * facing + (1 - over) * lax.rem(level + inward, deep)
        to_lane = lax.rem(lane + k // deep, 2)
        return lax.rem(side + over, 2) * half + to_level * 2 + to_lane

    def mate(i):
        return side * half + lax.rem(place + 1 + i, half)

    barrier = pltpu.get_barrier_semaphore()

    def greet(i, c):
        pl.semaphore_signal(
            barrier, inc=1, device_id=(peer(i), h), device_id_type=pl.DeviceIdType.MESH
        )
        return c

    lax.fori_loop(0, n - 1, greet, 0)
    for g in others:
        pl.semaphore_signal(barrier, inc=1, device_id=(me, g), device_id_type=pl.DeviceIdType.MESH)
    pl.semaphore_wait(barrier, n - 1 + 3)

    def tab_copy(s, dest):
        return remote(
            tab_ref, tabs.at[pl.ds(s * 8, 8)], tab_send.at[dest], tab_recv.at[s], dest, h
        )

    def tab_start(i, c):
        tab_copy(me, peer(i)).start()
        return c

    lax.fori_loop(0, n - 1, tab_start, 0)

    def to_right():
        return remote(
            kv_ref.at[blocks - 1], kvp.at[0], halo_send.at[0], halo_recv.at[0], lax.rem(me + 1, n), h
        )

    def to_left():
        return remote(
            kv_ref.at[0],
            kvp.at[blocks + 1],
            halo_send.at[1],
            halo_recv.at[1],
            lax.rem(me + n - 1, n),
            h,
        )

    def first_copy(dest):
        return remote(kv_ref.at[0], ends.at[0], first_send.at[dest], ends_recv.at[0], dest, h)

    def final_copy(dest):
        return remote(kv_ref.at[blocks - 1], ends.at[1], final_send.at[dest], ends_recv.at[1], dest, h)

    def first_relay(dest):
        return remote(ends.at[0], ends.at[0], first_send.at[dest], ends_recv.at[0], dest, h)

    def final_relay(dest):
        return remote(ends.at[1], ends.at[1], final_send.at[dest], ends_recv.at[1], dest, h)

    def to_mates(copy):
        def go(i, c):
            copy(mate(i)).start()
            return c

        lax.fori_loop(0, half - 1, go, 0)

    @pl.when(me == 0)
    def _():
        first_copy(half).start()
        to_mates(first_copy)
        ends[0] = kv_ref[0]
        kvp[0] = jnp.zeros_like(kvp[0])

    @pl.when(me == n - 1)
    def _():
        final_copy(half - 1).start()
        to_mates(final_copy)
        ends[1] = kv_ref[blocks - 1]
        kvp[blocks + 1] = jnp.zeros_like(kvp[0])

    @pl.when(me < n - 1)
    def _():
        to_right().start()

    @pl.when(me > 0)
    def _():
        to_left().start()

    odd = lax.rem(me, 2)

    def w_span(c):
        place_c = c + odd * (W_CHUNKS - 1 - 2 * c)
        return pl.ds(pl.multiple_of(place_c * w_rows, w_rows), w_rows)

    def w_piece(g, c):
        return wall.at[g, w_span(c)]

    def wx_copy(g, c):
        return remote(
            w_ref.at[w_span(c)],
            w_piece(g, c),
            wx_send.at[c],
            wx_recv.at[c],
            me,
            across,
        )

    for c in range(W_CHUNKS - 1):
        wx_copy(h, c).start()

    def tab_wait(i, c):
        tab_copy(peer(i), me).wait_recv()
        return c

    lax.fori_loop(0, n - 1, tab_wait, 0)
    tabs[pl.ds(pl.multiple_of(me * 8, 8), 8), :] = tab_ref[...]
    to_smem = pltpu.make_async_copy(tabs, tabs_s, tab_local)
    to_smem.start()
    to_smem.wait()

    @pl.when(me == half)
    def _():
        first_copy(me).wait_recv()
        to_mates(first_relay)

    @pl.when(me == half - 1)
    def _():
        final_copy(me).wait_recv()
        to_mates(final_relay)

    def rand_copy(hd, s, dest):
        return remote(
            stage.at[hd, dest],
            recvs[hd].at[s],
            rand_send.at[hd * n + dest],
            rand_recv.at[hd * n + s],
            dest,
            h,
        )

    def pick(buf, hd, dest):
        for k in range(slots):
            block = tabs_s[dest * 8, me * slots + k]
            buf[k, :, :HEAD_DIM] = kv_ref[block, :, pl.ds(hd * HEAD_DIM, HEAD_DIM)]
            buf[k, :, HEAD_DIM:] = kv_ref[block, :, pl.ds(feat + hd * HEAD_DIM, HEAD_DIM)]

    for hd in range(heads):

        def rand_start(i, c, hd=hd):
            dest = peer(i)
            pick(stage.at[hd, dest], hd, dest)
            rand_copy(hd, me, dest).start()
            return c

        lax.fori_loop(0, n - 1, rand_start, 0)
    for hd in range(heads):
        pick(recvs[hd].at[me], hd, me)

    w_own = pltpu.make_async_copy(w_ref, wall.at[h], w_local)
    w_own.start()
    ws_copy = remote(w_ref, wall.at[h], ws_send, ws_recv, me, sib)
    ws_copy.start()

    def fill(j, c):
        kvp[j + 1] = kv_ref[j]
        return c

    lax.fori_loop(0, blocks, fill, 0)

    @pl.when(me > 0)
    def _():
        to_right().wait_recv()

        @pl.when(me != half)
        def _():
            first_copy(me).wait_recv()

    @pl.when(me < n - 1)
    def _():
        to_left().wait_recv()

        @pl.when(me != half - 1)
        def _():
            final_copy(me).wait_recv()

    nt = (((1,), (1,)), ((), ()))

    def near(j, c):
        block = me * blocks + j
        rows = pl.ds(pl.multiple_of(j * BLOCK, BLOCK), BLOCK)
        b_prev = jnp.where(block >= 1, 0.0, NEG)
        b_next = jnp.where(block <= total_blocks - 2, 0.0, NEG)
        b_first = jnp.where(block >= 2, 0.0, NEG)
        b_final = jnp.where(block <= total_blocks - 3, 0.0, NEG)
        col = lax.broadcasted_iota(jnp.int32, (BLOCK, 3 * BLOCK), 1)
        b_win = jnp.where(col < BLOCK, b_prev, jnp.where(col >= 2 * BLOCK, b_next, 0.0))
        cole = lax.broadcasted_iota(jnp.int32, (BLOCK, 2 * BLOCK), 1)
        b_end = jnp.where(cole < BLOCK, b_first, b_final)
        for hd in range(heads):
            kc = pl.ds(hd * HEAD_DIM, HEAD_DIM)
            vc = pl.ds(feat + hd * HEAD_DIM, HEAD_DIM)
            qh = q_ref[rows, kc]
            kw = kvp[pl.ds(j, 3), :, kc].reshape(3 * BLOCK, HEAD_DIM)
            vw = kvp[pl.ds(j, 3), :, vc].reshape(3 * BLOCK, HEAD_DIM)
            ke = ends[:, :, kc].reshape(2 * BLOCK, HEAD_DIM)
            ve = ends[:, :, vc].reshape(2 * BLOCK, HEAD_DIM)
            sw = lax.dot_general(qh, kw, nt, preferred_element_type=jnp.float32) * scale + b_win
            se = lax.dot_general(qh, ke, nt, preferred_element_type=jnp.float32) * scale + b_end
            m = jnp.maximum(
                jnp.max(sw, axis=1, keepdims=True), jnp.max(se, axis=1, keepdims=True)
            )
            pw = jnp.exp(sw - m)
            pe = jnp.exp(se - m)
            tot = jnp.sum(pw, axis=1, keepdims=True) + jnp.sum(pe, axis=1, keepdims=True)
            o = jnp.dot(pw.astype(jnp.bfloat16), vw, preferred_element_type=jnp.float32)
            o = o + jnp.dot(pe.astype(jnp.bfloat16), ve, preferred_element_type=jnp.float32)
            m_ref[rows, kc] = jnp.broadcast_to(m, (BLOCK, HEAD_DIM))
            l_ref[rows, kc] = jnp.broadcast_to(tot, (BLOCK, HEAD_DIM))
            acc[rows, kc] = o
        return c

    lax.fori_loop(0, blocks, near, 0)

    def wf_copy(g, c):
        return remote(w_piece(g, c), w_piece(g, c), wf_send.at[c], wf_recv.at[c], me, sib)

    def wy_copy(span):
        return remote(wall.at[across, span], wall.at[across, span], wy_send, wy_recv, pair, h)

    last = W_CHUNKS - 1

    def rand_wait(hd):
        def go(i, c):
            rand_copy(hd, peer(i), me).wait_recv()
            return c

        lax.fori_loop(0, n - 1, go, 0)

    quarter = blocks // 4

    def att_copy(hd, t, g):
        return remote(
            att.at[hd, t], attr.at[hd, g], att_send.at[hd * 4 + t], att_recv.at[hd * 4 + g], me, t
        )

    def far(hd):
        kc = pl.ds(hd * HEAD_DIM, HEAD_DIM)

        def one(i, c):
            t = 2 * lax.rem(h // 2 + 1 + i // 2, 2) + lax.rem(h + i, 2)
            for u in range(quarter):
                j = t * quarter + u
                rows = pl.ds(pl.multiple_of(j * BLOCK, BLOCK), BLOCK)
                s0 = slot_ref[2 * j]
                s1 = slot_ref[2 * j + 1]
                col = lax.broadcasted_iota(jnp.int32, (BLOCK, 2 * BLOCK), 1)
                bias = jnp.where(col < BLOCK, bias_ref[2 * j], bias_ref[2 * j + 1])
                r0, k0 = s0 // slots, lax.rem(s0, slots)
                r1, k1 = s1 // slots, lax.rem(s1, slots)
                both = jnp.concatenate([recvs[hd][r0, k0], recvs[hd][r1, k1]], axis=0)
                keys, vals = both[:, :HEAD_DIM], both[:, HEAD_DIM:]
                s = lax.dot_general(q_ref[rows, kc], keys, nt, preferred_element_type=jnp.float32)
                s = s * scale + bias
                m0 = m_ref[rows, kc]
                m = jnp.maximum(m0, jnp.max(s, axis=1, keepdims=True))
                alpha = jnp.exp(m0 - m)
                p = jnp.exp(s - m)
                tot = l_ref[rows, kc] * alpha + jnp.sum(p, axis=1, keepdims=True)
                o = jnp.dot(p.astype(jnp.bfloat16), vals, preferred_element_type=jnp.float32)
                o = o + acc[rows, kc] * alpha
                att[hd, t, u * BLOCK : (u + 1) * BLOCK, :] = (o / tot).astype(jnp.bfloat16)

            @pl.when(i != 2)
            def _():
                att_copy(hd, t, h).start()

            return c

        lax.fori_loop(0, 4, one, 0)

    tile = 512
    tiles = out_ref.shape[1] // tile
    early = (heads - 1) * HEAD_DIM

    def joined(buf, g):
        return jnp.concatenate([buf[hd, g] for hd in range(heads - 1)], axis=1)

    def project_a(i, c):
        cols = pl.ds(pl.multiple_of(i * tile, tile), tile)
        o = jnp.dot(joined(att, h), wall[h, :early, cols], preferred_element_type=jnp.float32)
        for g in (sib, across, across_sib):
            o = o + jnp.dot(
                joined(attr, g), wall[g, :early, cols], preferred_element_type=jnp.float32
            )
        oacc[:, cols] = o
        return c

    def project_b(i, c):
        cols = pl.ds(pl.multiple_of(i * tile, tile), tile)
        o = oacc[:, cols]
        o = o + jnp.dot(att[last, h], wall[h, early:, cols], preferred_element_type=jnp.float32)
        for g in (sib, across, across_sib):
            o = o + jnp.dot(
                attr[last, g], wall[g, early:, cols], preferred_element_type=jnp.float32
            )
        out_ref[:, cols] = o.astype(jnp.bfloat16)
        return c

    for hd in range(heads):
        if hd < last:
            wx_copy(across, hd).wait_recv()
            wf_copy(across, hd).start()
        if hd == 0:
            wy_copy(w_span(0)).start()
        if hd == last:
            wy_copy(w_span(last)).wait_recv()
            wf_copy(across, last).start()
            w_own.wait()
            ws_copy.wait_recv()
            for c in range(W_CHUNKS):
                wf_copy(across_sib, c).wait_recv()
            for e in range(last):
                for g in others:
                    att_copy(e, h, g).wait_recv()
            lax.fori_loop(0, tiles, project_a, 0)
        rand_wait(hd)
        far(hd)

    for g in others:
        att_copy(last, h, g).wait_recv()
    lax.fori_loop(0, tiles, project_b, 0)

    def drain(i, c):
        tab_copy(me, peer(i)).wait_send()
        for hd in range(heads):
            rand_copy(hd, me, peer(i)).wait_send()
        return c

    lax.fori_loop(0, n - 1, drain, 0)

    def from_mates(copy):
        def go(i, c):
            copy(mate(i)).wait_send()
            return c

        lax.fori_loop(0, half - 1, go, 0)

    @pl.when(me == 0)
    def _():
        first_copy(half).wait_send()
        from_mates(first_copy)

    @pl.when(me == n - 1)
    def _():
        final_copy(half - 1).wait_send()
        from_mates(final_copy)

    @pl.when(me == half)
    def _():
        from_mates(first_relay)

    @pl.when(me == half - 1)
    def _():
        from_mates(final_relay)

    @pl.when(me < n - 1)
    def _():
        to_right().wait_send()

    @pl.when(me > 0)
    def _():
        to_left().wait_send()

    for c in range(W_CHUNKS):
        if c < last:
            wx_copy(h, c).wait_send()
        wf_copy(across, c).wait_send()
    wy_copy(w_span(0)).wait_send()
    ws_copy.wait_send()
    for hd in range(heads):
        for t in others:
            att_copy(hd, t, h).wait_send()


def body(queries, keys_values, rand_blocks, w_out):
    tok_rows, feat = queries.shape
    heads = feat // HEAD_DIM
    blocks = tok_rows // BLOCK
    n = lax.axis_size("seq")
    n_head = lax.axis_size("head")
    all_blocks = blocks * n
    position = lax.axis_index("seq")
    entries = rand_blocks.shape[0] * rand_blocks.shape[1]
    slots = max(1, entries // n)
    width = w_out.shape[1]

    flat = rand_blocks.reshape(entries)
    owner = flat // blocks
    offset = flat % blocks
    earlier = jnp.arange(entries)[:, None] > jnp.arange(entries)[None, :]
    rank = jnp.sum((owner[:, None] == owner[None, :]) & earlier, axis=1)
    slot = (owner * slots + rank).astype(jnp.int32)
    placed = slot[:, None] == jnp.arange(128)[None, :]
    outgoing = jnp.sum(jnp.where(placed, offset[:, None], 0), axis=0).astype(jnp.int32)
    table = jnp.broadcast_to(outgoing[None, :], (8, 128))

    ids = position * blocks + jnp.arange(blocks, dtype=jnp.int32)
    taken = [ids - 1, ids, ids + 1, jnp.zeros_like(ids), jnp.zeros_like(ids) + (all_blocks - 1)]
    flags = []
    for column in range(rand_blocks.shape[1]):
        chosen = rand_blocks[:, column]
        flags.append(reduce(jnp.logical_or, [chosen == other for other in taken]))
        taken.append(chosen)
    bias = jnp.where(jnp.stack(flags, axis=1), NEG, 0.0).astype(jnp.float32).reshape(entries)

    kv = keys_values.reshape(blocks, BLOCK, 2 * feat)
    vmem = pl.BlockSpec(memory_space=pltpu.VMEM)
    smem = pl.BlockSpec(memory_space=pltpu.SMEM)
    bf16, f32, i32 = jnp.bfloat16, jnp.float32, jnp.int32
    rows_out = tok_rows // n_head
    dma = pltpu.SemaphoreType.DMA
    return pl.pallas_call(
        functools.partial(kernel, n, slots, blocks, heads),
        out_shape=jax.ShapeDtypeStruct((rows_out, width), bf16),
        in_specs=[vmem, vmem, vmem, smem, smem, pl.BlockSpec(memory_space=pl.ANY)],
        out_specs=vmem,
        scratch_shapes=[
            pltpu.VMEM((blocks + 2, BLOCK, 2 * feat), bf16),
            pltpu.VMEM((2, BLOCK, 2 * feat), bf16),
            pltpu.VMEM((n * 8, 128), i32),
            pltpu.SMEM((n * 8, 128), i32),
            pltpu.VMEM((heads, n, slots, BLOCK, 2 * HEAD_DIM), bf16),
            *[pltpu.VMEM((n, slots, BLOCK, 2 * HEAD_DIM), bf16)] * 4,
            pltpu.VMEM((tok_rows, feat), f32),
            pltpu.VMEM((tok_rows, feat), f32),
            pltpu.VMEM((tok_rows, feat), f32),
            pltpu.VMEM((heads, n_head, rows_out, HEAD_DIM), bf16),
            pltpu.VMEM((heads, n_head, rows_out, HEAD_DIM), bf16),
            pltpu.VMEM((n_head, feat, width), bf16),
            pltpu.VMEM((rows_out, width), f32),
            dma((n,)),
            dma((n,)),
            dma,
            dma((2,)),
            dma((2,)),
            dma((n,)),
            dma((n,)),
            dma((2,)),
            dma((heads * n,)),
            dma((heads * n,)),
            dma,
            dma((W_CHUNKS,)),
            dma((W_CHUNKS,)),
            dma,
            dma,
            dma((W_CHUNKS,)),
            dma((W_CHUNKS,)),
            dma,
            dma,
            dma((heads * n_head,)),
            dma((heads * n_head,)),
        ],
        compiler_params=pltpu.CompilerParams(
            collective_id=0, has_side_effects=True, vmem_limit_bytes=60 * 1024 * 1024
        ),
        cost_estimate=pl.CostEstimate(
            flops=6_000_000_000, bytes_accessed=20_000_000, transcendentals=2_000_000
        ),
    )(queries, kv, table, slot, bias, w_out)


def solution(mesh):
    in_specs = (P("seq", "head"), P("seq", None, "head"), P("seq", None), P("head", None))
    out_specs = P(("seq", "head"), None)
    return jax.shard_map(body, mesh=mesh, in_specs=in_specs, out_specs=out_specs, check_vma=False)
```

```python
import functools

import jax
import jax.numpy as jnp
from jax import lax
from jax.experimental import pallas as pl
from jax.experimental.pallas import tpu as pltpu
from jax.sharding import PartitionSpec as P

HEAD_DIM = 128
BLOCK = 64
W_CHUNKS = 4
NEG = -1e30


def kernel(
    n,
    slots,
    blocks,
    heads,
    q_hbm,
    raw_hbm,
    rb_ref,
    w_ref,
    out_ref,
    q_ref,
    raw_ref,
    kv_ref,
    tab_ref,
    out_v,
    in_sem,
    out_sem,
    kvp,
    ends,
    tabs,
    tabs_s,
    stage,
    recv_0,
    recv_1,
    recv_2,
    recv_3,
    m_ref,
    l_ref,
    acc,
    att,
    attr,
    wall,
    oacc,
    tab_send,
    tab_recv,
    tab_local,
    halo_send,
    halo_recv,
    first_send,
    final_send,
    ends_recv,
    rand_send,
    rand_recv,
    w_local,
    wx_send,
    wx_recv,
    ws_send,
    ws_recv,
    wf_send,
    wf_recv,
    wy_send,
    wy_recv,
    att_send,
    att_recv,
):
    recvs = (recv_0, recv_1, recv_2, recv_3)
    me = lax.axis_index("seq")
    h = lax.axis_index("head")
    sib = h + 1 - 2 * lax.rem(h, 2)
    across = lax.rem(h + 2, 4)
    across_sib = lax.rem(sib + 2, 4)
    others = (across, across_sib, sib)
    total_blocks = n * blocks
    scale = HEAD_DIM ** (-0.5)
    w_rows = w_ref.shape[0] // W_CHUNKS
    feat = heads * HEAD_DIM

    def remote(src, dst, ssem, rsem, seq, head):
        return pltpu.make_async_remote_copy(
            src_ref=src,
            dst_ref=dst,
            send_sem=ssem,
            recv_sem=rsem,
            device_id=(seq, head),
            device_id_type=pl.DeviceIdType.MESH,
        )

    half = n // 2
    side, place = me // half, lax.rem(me, half)
    pair = me + 1 - 2 * lax.rem(me, 2)

    deep = half // 2
    level, lane = place // 2, lax.rem(place, 2)

    def peer(i):
        over = 1 - lax.rem(i, 2)
        k = (i + 1) // 2
        inward = lax.rem(k, deep)
        facing = inward + (1 - side) * (deep - 1 - 2 * inward)
        to_level = over * facing + (1 - over) * lax.rem(level + inward, deep)
        to_lane = lax.rem(lane + k // deep, 2)
        return lax.rem(side + over, 2) * half + to_level * 2 + to_lane

    def mate(i):
        return side * half + lax.rem(place + 1 + i, half)

    load_raw = pltpu.make_async_copy(raw_hbm, raw_ref, in_sem.at[0])
    load_q = pltpu.make_async_copy(q_hbm, q_ref, in_sem.at[1])
    load_raw.start()
    load_q.start()

    barrier = pltpu.get_barrier_semaphore()

    def greet(i, c):
        pl.semaphore_signal(
            barrier, inc=1, device_id=(peer(i), h), device_id_type=pl.DeviceIdType.MESH
        )
        return c

    lax.fori_loop(0, n - 1, greet, 0)
    for g in others:
        pl.semaphore_signal(barrier, inc=1, device_id=(me, g), device_id_type=pl.DeviceIdType.MESH)
    entries = 2 * blocks
    lanes = lax.broadcasted_iota(jnp.int32, (entries, 128), 1)
    subs = lax.broadcasted_iota(jnp.int32, (entries, 128), 0)
    owner_row = jnp.full((entries, 128), -1, jnp.int32)
    owner_col = jnp.zeros((entries, 128), jnp.int32)
    offset_col = jnp.zeros((entries, 128), jnp.int32)
    for e in range(entries):
        named = rb_ref[e % 2, e // 2]
        owner = named // blocks
        owner_row = jnp.where(lanes == e, owner, owner_row)
        owner_col = jnp.where(subs == e, owner, owner_col)
        offset_col = jnp.where(subs == e, named - owner * blocks, offset_col)
    ahead = jnp.where((owner_row == owner_col) & (lanes < subs), 1, 0)
    slot_col = owner_col * slots + jnp.sum(ahead, axis=1, keepdims=True)
    outgoing = jnp.sum(jnp.where(slot_col == lanes, offset_col, 0), axis=0, keepdims=True)
    tab_ref[...] = jnp.broadcast_to(outgoing, (8, 128))
    tabs[n * 8 : n * 8 + entries, :] = slot_col

    pl.semaphore_wait(barrier, n - 1 + 3)

    def tab_copy(s, dest):
        return remote(
            tab_ref, tabs.at[pl.ds(s * 8, 8)], tab_send.at[dest], tab_recv.at[s], dest, h
        )

    def tab_start(i, c):
        tab_copy(me, peer(i)).start()
        return c

    lax.fori_loop(0, n - 1, tab_start, 0)

    load_raw.wait()

    def unpack(j):
        kv_ref[j, :, :feat] = raw_ref[j, :, 0, :]
        kv_ref[j, :, feat:] = raw_ref[j, :, 1, :]

    unpack(0)
    unpack(blocks - 1)

    def to_right():
        return remote(
            kv_ref.at[blocks - 1], kvp.at[0], halo_send.at[0], halo_recv.at[0], lax.rem(me + 1, n), h
        )

    def to_left():
        return remote(
            kv_ref.at[0],
            kvp.at[blocks + 1],
            halo_send.at[1],
            halo_recv.at[1],
            lax.rem(me + n - 1, n),
            h,
        )

    def first_copy(dest):
        return remote(kv_ref.at[0], ends.at[0], first_send.at[dest], ends_recv.at[0], dest, h)

    def final_copy(dest):
        return remote(kv_ref.at[blocks - 1], ends.at[1], final_send.at[dest], ends_recv.at[1], dest, h)

    def first_relay(dest):
        return remote(ends.at[0], ends.at[0], first_send.at[dest], ends_recv.at[0], dest, h)

    def final_relay(dest):
        return remote(ends.at[1], ends.at[1], final_send.at[dest], ends_recv.at[1], dest, h)

    def to_mates(copy):
        def go(i, c):
            copy(mate(i)).start()
            return c

        lax.fori_loop(0, half - 1, go, 0)

    @pl.when(me == 0)
    def _():
        first_copy(half).start()
        to_mates(first_copy)
        ends[0] = kv_ref[0]
        kvp[0] = jnp.zeros_like(kvp[0])

    @pl.when(me == n - 1)
    def _():
        final_copy(half - 1).start()
        to_mates(final_copy)
        ends[1] = kv_ref[blocks - 1]
        kvp[blocks + 1] = jnp.zeros_like(kvp[0])

    @pl.when(me < n - 1)
    def _():
        to_right().start()

    @pl.when(me > 0)
    def _():
        to_left().start()

    def unpack_one(j, c):
        unpack(j)
        return c

    lax.fori_loop(1, blocks - 1, unpack_one, 0)

    odd = lax.rem(me, 2)

    def w_span(c):
        place_c = c + odd * (W_CHUNKS - 1 - 2 * c)
        return pl.ds(pl.multiple_of(place_c * w_rows, w_rows), w_rows)

    def w_piece(g, c):
        return wall.at[g, w_span(c)]

    def wx_copy(g, c):
        return remote(
            w_ref.at[w_span(c)],
            w_piece(g, c),
            wx_send.at[c],
            wx_recv.at[c],
            me,
            across,
        )

    for c in range(W_CHUNKS - 1):
        wx_copy(h, c).start()

    def tab_wait(i, c):
        tab_copy(peer(i), me).wait_recv()
        return c

    lax.fori_loop(0, n - 1, tab_wait, 0)
    tabs[pl.ds(pl.multiple_of(me * 8, 8), 8), :] = tab_ref[...]
    to_smem = pltpu.make_async_copy(tabs, tabs_s, tab_local)
    to_smem.start()
    to_smem.wait()

    @pl.when(me == half)
    def _():
        first_copy(me).wait_recv()
        to_mates(first_relay)

    @pl.when(me == half - 1)
    def _():
        final_copy(me).wait_recv()
        to_mates(final_relay)

    def rand_copy(hd, s, dest):
        return remote(
            stage.at[hd, dest],
            recvs[hd].at[s],
            rand_send.at[hd * n + dest],
            rand_recv.at[hd * n + s],
            dest,
            h,
        )

    def pick(buf, hd, dest):
        for k in range(slots):
            block = tabs_s[dest * 8, me * slots + k]
            buf[k, :, :HEAD_DIM] = kv_ref[block, :, pl.ds(hd * HEAD_DIM, HEAD_DIM)]
            buf[k, :, HEAD_DIM:] = kv_ref[block, :, pl.ds(feat + hd * HEAD_DIM, HEAD_DIM)]

    for hd in range(heads):

        def rand_start(i, c, hd=hd):
            dest = peer(i)
            pick(stage.at[hd, dest], hd, dest)
            rand_copy(hd, me, dest).start()
            return c

        lax.fori_loop(0, n - 1, rand_start, 0)
    for hd in range(heads):
        pick(recvs[hd].at[me], hd, me)

    w_own = pltpu.make_async_copy(w_ref, wall.at[h], w_local)
    w_own.start()
    ws_copy = remote(w_ref, wall.at[h], ws_send, ws_recv, me, sib)
    ws_copy.start()

    def fill(j, c):
        kvp[j + 1] = kv_ref[j]
        return c

    lax.fori_loop(0, blocks, fill, 0)
    load_q.wait()

    @pl.when(me > 0)
    def _():
        to_right().wait_recv()

        @pl.when(me != half)
        def _():
            first_copy(me).wait_recv()

    @pl.when(me < n - 1)
    def _():
        to_left().wait_recv()

        @pl.when(me != half - 1)
        def _():
            final_copy(me).wait_recv()

    nt = (((1,), (1,)), ((), ()))

    def near(j, c):
        block = me * blocks + j
        rows = pl.ds(pl.multiple_of(j * BLOCK, BLOCK), BLOCK)
        b_prev = jnp.where(block >= 1, 0.0, NEG)
        b_next = jnp.where(block <= total_blocks - 2, 0.0, NEG)
        b_first = jnp.where(block >= 2, 0.0, NEG)
        b_final = jnp.where(block <= total_blocks - 3, 0.0, NEG)
        col = lax.broadcasted_iota(jnp.int32, (BLOCK, 3 * BLOCK), 1)
        b_win = jnp.where(col < BLOCK, b_prev, jnp.where(col >= 2 * BLOCK, b_next, 0.0))
        cole = lax.broadcasted_iota(jnp.int32, (BLOCK, 2 * BLOCK), 1)
        b_end = jnp.where(cole < BLOCK, b_first, b_final)
        for hd in range(heads):
            kc = pl.ds(hd * HEAD_DIM, HEAD_DIM)
            vc = pl.ds(feat + hd * HEAD_DIM, HEAD_DIM)
            qh = q_ref[rows, kc]
            kw = kvp[pl.ds(j, 3), :, kc].reshape(3 * BLOCK, HEAD_DIM)
            vw = kvp[pl.ds(j, 3), :, vc].reshape(3 * BLOCK, HEAD_DIM)
            ke = ends[:, :, kc].reshape(2 * BLOCK, HEAD_DIM)
            ve = ends[:, :, vc].reshape(2 * BLOCK, HEAD_DIM)
            sw = lax.dot_general(qh, kw, nt, preferred_element_type=jnp.float32) * scale + b_win
            se = lax.dot_general(qh, ke, nt, preferred_element_type=jnp.float32) * scale + b_end
            m = jnp.maximum(
                jnp.max(sw, axis=1, keepdims=True), jnp.max(se, axis=1, keepdims=True)
            )
            pw = jnp.exp(sw - m)
            pe = jnp.exp(se - m)
            tot = jnp.sum(pw, axis=1, keepdims=True) + jnp.sum(pe, axis=1, keepdims=True)
            o = jnp.dot(pw.astype(jnp.bfloat16), vw, preferred_element_type=jnp.float32)
            o = o + jnp.dot(pe.astype(jnp.bfloat16), ve, preferred_element_type=jnp.float32)
            m_ref[rows, kc] = jnp.broadcast_to(m, (BLOCK, HEAD_DIM))
            l_ref[rows, kc] = jnp.broadcast_to(tot, (BLOCK, HEAD_DIM))
            acc[rows, kc] = o
        return c

    lax.fori_loop(0, blocks, near, 0)

    def wf_copy(g, c):
        return remote(w_piece(g, c), w_piece(g, c), wf_send.at[c], wf_recv.at[c], me, sib)

    def wy_copy(span):
        return remote(wall.at[across, span], wall.at[across, span], wy_send, wy_recv, pair, h)

    last = W_CHUNKS - 1

    def rand_wait(hd):
        def go(i, c):
            rand_copy(hd, peer(i), me).wait_recv()
            return c

        lax.fori_loop(0, n - 1, go, 0)

    quarter = blocks // 4

    def att_copy(hd, t, g):
        return remote(
            att.at[hd, t], attr.at[hd, g], att_send.at[hd * 4 + t], att_recv.at[hd * 4 + g], me, t
        )

    def far(hd):
        kc = pl.ds(hd * HEAD_DIM, HEAD_DIM)

        def one(i, c):
            t = 2 * lax.rem(h // 2 + 1 + i // 2, 2) + lax.rem(h + i, 2)
            for u in range(quarter):
                j = t * quarter + u
                rows = pl.ds(pl.multiple_of(j * BLOCK, BLOCK), BLOCK)
                s0 = tabs_s[n * 8 + 2 * j, 0]
                s1 = tabs_s[n * 8 + 2 * j + 1, 0]
                block = me * blocks + j
                n0, n1 = rb_ref[0, j], rb_ref[1, j]

                def clash(x, block=block):
                    near_by = (x >= block - 1) & (x <= block + 1)
                    return near_by | (x == 0) | (x == total_blocks - 1)

                b0 = jnp.where(clash(n0), NEG, 0.0)
                b1 = jnp.where(clash(n1) | (n1 == n0), NEG, 0.0)
                col = lax.broadcasted_iota(jnp.int32, (BLOCK, 2 * BLOCK), 1)
                bias = jnp.where(col < BLOCK, b0, b1)
                r0, k0 = s0 // slots, lax.rem(s0, slots)
                r1, k1 = s1 // slots, lax.rem(s1, slots)
                both = jnp.concatenate([recvs[hd][r0, k0], recvs[hd][r1, k1]], axis=0)
                keys, vals = both[:, :HEAD_DIM], both[:, HEAD_DIM:]
                s = lax.dot_general(q_ref[rows, kc], keys, nt, preferred_element_type=jnp.float32)
                s = s * scale + bias
                m0 = m_ref[rows, kc]
                m = jnp.maximum(m0, jnp.max(s, axis=1, keepdims=True))
                alpha = jnp.exp(m0 - m)
                p = jnp.exp(s - m)
                tot = l_ref[rows, kc] * alpha + jnp.sum(p, axis=1, keepdims=True)
                o = jnp.dot(p.astype(jnp.bfloat16), vals, preferred_element_type=jnp.float32)
                o = o + acc[rows, kc] * alpha
                att[hd, t, u * BLOCK : (u + 1) * BLOCK, :] = (o / tot).astype(jnp.bfloat16)

            @pl.when(i != 2)
            def _():
                att_copy(hd, t, h).start()

            return c

        lax.fori_loop(0, 4, one, 0)

    tile = 512
    tiles = out_ref.shape[1] // tile
    early = (heads - 1) * HEAD_DIM

    def joined(buf, g):
        return jnp.concatenate([buf[hd, g] for hd in range(heads - 1)], axis=1)

    def project_a(i, c):
        cols = pl.ds(pl.multiple_of(i * tile, tile), tile)
        o = jnp.dot(joined(att, h), wall[h, :early, cols], preferred_element_type=jnp.float32)
        for g in (sib, across, across_sib):
            o = o + jnp.dot(
                joined(attr, g), wall[g, :early, cols], preferred_element_type=jnp.float32
            )
        oacc[:, cols] = o
        return c

    def tail(bufs, cols):
        rows = jnp.concatenate([buf[last, g] for buf, g in bufs], axis=1)
        weights = jnp.concatenate([wall[g, early:, cols] for buf, g in bufs], axis=0)
        return oacc[:, cols] + jnp.dot(rows, weights, preferred_element_type=jnp.float32)

    def project_b(i, c):
        cols = pl.ds(pl.multiple_of(i * tile, tile), tile)
        oacc[:, cols] = tail(((att, h), (attr, sib)), cols)
        return c

    def out_copy(i):
        cols = pl.ds(pl.multiple_of(i * tile, tile), tile)
        return pltpu.make_async_copy(out_v.at[:, cols], out_ref.at[:, cols], out_sem.at[i])

    def project_c(i, c):
        cols = pl.ds(pl.multiple_of(i * tile, tile), tile)
        o = tail(((attr, across), (attr, across_sib)), cols)
        out_v[:, cols] = o.astype(jnp.bfloat16)
        out_copy(i).start()
        return c

    def out_wait(i, c):
        out_copy(i).wait()
        return c

    for hd in range(heads):
        if hd < last:
            wx_copy(across, hd).wait_recv()
            wf_copy(across, hd).start()
        if hd == 0:
            wy_copy(w_span(0)).start()
        if hd == last:
            wy_copy(w_span(last)).wait_recv()
            wf_copy(across, last).start()
            w_own.wait()
            ws_copy.wait_recv()
            for c in range(W_CHUNKS):
                wf_copy(across_sib, c).wait_recv()
            for e in range(last):
                for g in others:
                    att_copy(e, h, g).wait_recv()
            lax.fori_loop(0, tiles, project_a, 0)
        rand_wait(hd)
        far(hd)

    att_copy(last, h, sib).wait_recv()
    lax.fori_loop(0, tiles, project_b, 0)
    att_copy(last, h, across).wait_recv()
    att_copy(last, h, across_sib).wait_recv()
    lax.fori_loop(0, tiles, project_c, 0)

    def drain(i, c):
        tab_copy(me, peer(i)).wait_send()
        for hd in range(heads):
            rand_copy(hd, me, peer(i)).wait_send()
        return c

    lax.fori_loop(0, n - 1, drain, 0)

    def from_mates(copy):
        def go(i, c):
            copy(mate(i)).wait_send()
            return c

        lax.fori_loop(0, half - 1, go, 0)

    @pl.when(me == 0)
    def _():
        first_copy(half).wait_send()
        from_mates(first_copy)

    @pl.when(me == n - 1)
    def _():
        final_copy(half - 1).wait_send()
        from_mates(final_copy)

    @pl.when(me == half)
    def _():
        from_mates(first_relay)

    @pl.when(me == half - 1)
    def _():
        from_mates(final_relay)

    @pl.when(me < n - 1)
    def _():
        to_right().wait_send()

    @pl.when(me > 0)
    def _():
        to_left().wait_send()

    for c in range(W_CHUNKS):
        if c < last:
            wx_copy(h, c).wait_send()
        wf_copy(across, c).wait_send()
    wy_copy(w_span(0)).wait_send()
    ws_copy.wait_send()
    for hd in range(heads):
        for t in others:
            att_copy(hd, t, h).wait_send()
    lax.fori_loop(0, tiles, out_wait, 0)


def body(queries, keys_values, rand_blocks, w_out):
    tok_rows, feat = queries.shape
    heads = feat // HEAD_DIM
    blocks = tok_rows // BLOCK
    n = lax.axis_size("seq")
    n_head = lax.axis_size("head")
    entries = rand_blocks.shape[0] * rand_blocks.shape[1]
    slots = max(1, entries // n)
    width = w_out.shape[1]
    kv = keys_values.reshape(blocks, BLOCK, 2, feat)
    anywhere = pl.BlockSpec(memory_space=pl.ANY)
    bf16, f32, i32 = jnp.bfloat16, jnp.float32, jnp.int32
    rows_out = tok_rows // n_head
    dma = pltpu.SemaphoreType.DMA
    return pl.pallas_call(
        functools.partial(kernel, n, slots, blocks, heads),
        out_shape=jax.ShapeDtypeStruct((rows_out, width), bf16),
        in_specs=[anywhere, anywhere, pl.BlockSpec(memory_space=pltpu.SMEM), anywhere],
        out_specs=anywhere,
        scratch_shapes=[
            pltpu.VMEM((tok_rows, feat), bf16),
            pltpu.VMEM((blocks, BLOCK, 2, feat), bf16),
            pltpu.VMEM((blocks, BLOCK, 2 * feat), bf16),
            pltpu.VMEM((8, 128), i32),
            pltpu.VMEM((rows_out, width), bf16),
            dma((2,)),
            dma((width // 512,)),
            pltpu.VMEM((blocks + 2, BLOCK, 2 * feat), bf16),
            pltpu.VMEM((2, BLOCK, 2 * feat), bf16),
            pltpu.VMEM((n * 8 + entries, 128), i32),
            pltpu.SMEM((n * 8 + entries, 128), i32),
            pltpu.VMEM((heads, n, slots, BLOCK, 2 * HEAD_DIM), bf16),
            *[pltpu.VMEM((n, slots, BLOCK, 2 * HEAD_DIM), bf16)] * 4,
            pltpu.VMEM((tok_rows, feat), f32),
            pltpu.VMEM((tok_rows, feat), f32),
            pltpu.VMEM((tok_rows, feat), f32),
            pltpu.VMEM((heads, n_head, rows_out, HEAD_DIM), bf16),
            pltpu.VMEM((heads, n_head, rows_out, HEAD_DIM), bf16),
            pltpu.VMEM((n_head, feat, width), bf16),
            pltpu.VMEM((rows_out, width), f32),
            dma((n,)),
            dma((n,)),
            dma,
            dma((2,)),
            dma((2,)),
            dma((n,)),
            dma((n,)),
            dma((2,)),
            dma((heads * n,)),
            dma((heads * n,)),
            dma,
            dma((W_CHUNKS,)),
            dma((W_CHUNKS,)),
            dma,
            dma,
            dma((W_CHUNKS,)),
            dma((W_CHUNKS,)),
            dma,
            dma,
            dma((heads * n_head,)),
            dma((heads * n_head,)),
        ],
        compiler_params=pltpu.CompilerParams(
            collective_id=0, has_side_effects=True, vmem_limit_bytes=60 * 1024 * 1024
        ),
        cost_estimate=pl.CostEstimate(
            flops=6_000_000_000, bytes_accessed=20_000_000, transcendentals=2_000_000
        ),
    )(queries, kv, rand_blocks.T, w_out)


def solution(mesh):
    in_specs = (P("seq", "head"), P("seq", None, "head"), P("seq", None), P("head", None))
    out_specs = P(("seq", "head"), None)
    return jax.shard_map(body, mesh=mesh, in_specs=in_specs, out_specs=out_specs, check_vma=False)
```

```python
import functools

import jax
import jax.numpy as jnp
from jax import lax
from jax.experimental import pallas as pl
from jax.experimental.pallas import tpu as pltpu
from jax.sharding import PartitionSpec as P

HEAD_DIM = 128
BLOCK = 64
W_CHUNKS = 4
NEG = -1e30


def kernel(
    n,
    slots,
    blocks,
    heads,
    q_hbm,
    raw_hbm,
    rb_ref,
    w_ref,
    out_ref,
    q_ref,
    raw_ref,
    kv_ref,
    tab_ref,
    out_v,
    in_sem,
    out_sem,
    kvp,
    ends,
    tabs,
    tabs_s,
    stage,
    recv_0,
    recv_1,
    recv_2,
    recv_3,
    recv_4,
    stage_3,
    stage_4,
    p_ref,
    m_ref,
    l_ref,
    acc,
    att,
    attr,
    wall,
    oacc,
    tab_send,
    tab_recv,
    tab_local,
    halo_send,
    halo_recv,
    first_send,
    final_send,
    ends_recv,
    rand_send,
    rand_recv,
    w_local,
    wx_send,
    wx_recv,
    ws_send,
    ws_recv,
    wf_send,
    wf_recv,
    wy_send,
    wy_recv,
    att_send,
    att_recv,
):
    recvs = (recv_0, recv_1, recv_2, recv_3, recv_4)
    stages = (stage.at[0], stage.at[1], stage.at[2], stage_3, stage_4)
    parts = heads + 1
    last = heads - 1
    me = lax.axis_index("seq")
    h = lax.axis_index("head")
    sib = h + 1 - 2 * lax.rem(h, 2)
    across = lax.rem(h + 2, 4)
    across_sib = lax.rem(sib + 2, 4)
    others = (across, across_sib, sib)
    total_blocks = n * blocks
    scale = HEAD_DIM ** (-0.5)
    w_rows = w_ref.shape[0] // W_CHUNKS
    feat = heads * HEAD_DIM

    def remote(src, dst, ssem, rsem, seq, head):
        return pltpu.make_async_remote_copy(
            src_ref=src,
            dst_ref=dst,
            send_sem=ssem,
            recv_sem=rsem,
            device_id=(seq, head),
            device_id_type=pl.DeviceIdType.MESH,
        )

    half = n // 2
    side, place = me // half, lax.rem(me, half)
    pair = me + 1 - 2 * lax.rem(me, 2)

    deep = half // 2
    level, lane = place // 2, lax.rem(place, 2)

    def peer(i):
        over = 1 - lax.rem(i, 2)
        k = (i + 1) // 2
        inward = lax.rem(k, deep)
        facing = inward + (1 - side) * (deep - 1 - 2 * inward)
        to_level = over * facing + (1 - over) * lax.rem(level + inward, deep)
        to_lane = lax.rem(lane + k // deep, 2)
        return lax.rem(side + over, 2) * half + to_level * 2 + to_lane

    def mate(i):
        return side * half + lax.rem(place + 1 + i, half)

    load_raw = pltpu.make_async_copy(raw_hbm, raw_ref, in_sem.at[0])
    load_q = pltpu.make_async_copy(q_hbm, q_ref, in_sem.at[1])
    load_raw.start()
    load_q.start()

    barrier = pltpu.get_barrier_semaphore()

    def greet(i, c):
        pl.semaphore_signal(
            barrier, inc=1, device_id=(peer(i), h), device_id_type=pl.DeviceIdType.MESH
        )
        return c

    lax.fori_loop(0, n - 1, greet, 0)
    for g in others:
        pl.semaphore_signal(barrier, inc=1, device_id=(me, g), device_id_type=pl.DeviceIdType.MESH)
    entries = 2 * blocks
    lanes = lax.broadcasted_iota(jnp.int32, (entries, 128), 1)
    subs = lax.broadcasted_iota(jnp.int32, (entries, 128), 0)
    owner_row = jnp.full((entries, 128), -1, jnp.int32)
    owner_col = jnp.zeros((entries, 128), jnp.int32)
    offset_col = jnp.zeros((entries, 128), jnp.int32)
    for e in range(entries):
        named = rb_ref[e % 2, e // 2]
        owner = named // blocks
        owner_row = jnp.where(lanes == e, owner, owner_row)
        owner_col = jnp.where(subs == e, owner, owner_col)
        offset_col = jnp.where(subs == e, named - owner * blocks, offset_col)
    ahead = jnp.where((owner_row == owner_col) & (lanes < subs), 1, 0)
    slot_col = owner_col * slots + jnp.sum(ahead, axis=1, keepdims=True)
    outgoing = jnp.sum(jnp.where(slot_col == lanes, offset_col, 0), axis=0, keepdims=True)
    tab_ref[...] = jnp.broadcast_to(outgoing, (8, 128))
    tabs[n * 8 : n * 8 + entries, :] = slot_col

    pl.semaphore_wait(barrier, n - 1 + 3)

    def tab_copy(s, dest):
        return remote(
            tab_ref, tabs.at[pl.ds(s * 8, 8)], tab_send.at[dest], tab_recv.at[s], dest, h
        )

    def tab_start(i, c):
        tab_copy(me, peer(i)).start()
        return c

    lax.fori_loop(0, n - 1, tab_start, 0)

    load_raw.wait()

    def unpack(j):
        kv_ref[j, :, :feat] = raw_ref[j, :, 0, :]
        kv_ref[j, :, feat:] = raw_ref[j, :, 1, :]

    unpack(0)
    unpack(blocks - 1)

    def to_right():
        return remote(
            kv_ref.at[blocks - 1], kvp.at[0], halo_send.at[0], halo_recv.at[0], lax.rem(me + 1, n), h
        )

    def to_left():
        return remote(
            kv_ref.at[0],
            kvp.at[blocks + 1],
            halo_send.at[1],
            halo_recv.at[1],
            lax.rem(me + n - 1, n),
            h,
        )

    def first_copy(dest):
        return remote(kv_ref.at[0], ends.at[0], first_send.at[dest], ends_recv.at[0], dest, h)

    def final_copy(dest):
        return remote(kv_ref.at[blocks - 1], ends.at[1], final_send.at[dest], ends_recv.at[1], dest, h)

    def first_relay(dest):
        return remote(ends.at[0], ends.at[0], first_send.at[dest], ends_recv.at[0], dest, h)

    def final_relay(dest):
        return remote(ends.at[1], ends.at[1], final_send.at[dest], ends_recv.at[1], dest, h)

    def to_mates(copy):
        def go(i, c):
            copy(mate(i)).start()
            return c

        lax.fori_loop(0, half - 1, go, 0)

    @pl.when(me == 0)
    def _():
        first_copy(half).start()
        to_mates(first_copy)
        ends[0] = kv_ref[0]
        kvp[0] = jnp.zeros_like(kvp[0])

    @pl.when(me == n - 1)
    def _():
        final_copy(half - 1).start()
        to_mates(final_copy)
        ends[1] = kv_ref[blocks - 1]
        kvp[blocks + 1] = jnp.zeros_like(kvp[0])

    @pl.when(me < n - 1)
    def _():
        to_right().start()

    @pl.when(me > 0)
    def _():
        to_left().start()

    def unpack_one(j, c):
        unpack(j)
        return c

    lax.fori_loop(1, blocks - 1, unpack_one, 0)

    odd = lax.rem(me, 2)

    def w_span(c):
        place_c = c + odd * (W_CHUNKS - 1 - 2 * c)
        return pl.ds(pl.multiple_of(place_c * w_rows, w_rows), w_rows)

    def w_piece(g, c):
        return wall.at[g, w_span(c)]

    def wx_copy(g, c):
        return remote(
            w_ref.at[w_span(c)],
            w_piece(g, c),
            wx_send.at[c],
            wx_recv.at[c],
            me,
            across,
        )

    for c in range(W_CHUNKS - 1):
        wx_copy(h, c).start()

    def tab_wait(i, c):
        tab_copy(peer(i), me).wait_recv()
        return c

    lax.fori_loop(0, n - 1, tab_wait, 0)
    tabs[pl.ds(pl.multiple_of(me * 8, 8), 8), :] = tab_ref[...]
    to_smem = pltpu.make_async_copy(tabs, tabs_s, tab_local)
    to_smem.start()
    to_smem.wait()

    @pl.when(me == half)
    def _():
        first_copy(me).wait_recv()
        to_mates(first_relay)

    @pl.when(me == half - 1)
    def _():
        final_copy(me).wait_recv()
        to_mates(final_relay)

    def rand_copy(hd, s, dest):
        return remote(
            stages[hd].at[dest],
            recvs[hd].at[s],
            rand_send.at[hd * n + dest],
            rand_recv.at[hd * n + s],
            dest,
            h,
        )

    def pick(buf, part, dest):
        hd = min(part, last)
        for k in range(slots):
            block = tabs_s[dest * 8, me * slots + k]
            keys = kv_ref[block, :, pl.ds(hd * HEAD_DIM, HEAD_DIM)]
            vals = kv_ref[block, :, pl.ds(feat + hd * HEAD_DIM, HEAD_DIM)]
            if part < last:
                buf[k, :, :HEAD_DIM] = keys
                buf[k, :, HEAD_DIM:] = vals
            else:
                buf[k] = keys if part == last else vals

    for hd in range(parts):

        def rand_start(i, c, hd=hd):
            dest = peer(i)
            pick(stages[hd].at[dest], hd, dest)
            rand_copy(hd, me, dest).start()
            return c

        lax.fori_loop(0, n - 1, rand_start, 0)
    for hd in range(parts):
        pick(recvs[hd].at[me], hd, me)

    w_own = pltpu.make_async_copy(w_ref, wall.at[h], w_local)
    w_own.start()
    ws_copy = remote(w_ref, wall.at[h], ws_send, ws_recv, me, sib)
    ws_copy.start()

    def fill(j, c):
        kvp[j + 1] = kv_ref[j]
        return c

    lax.fori_loop(0, blocks, fill, 0)
    load_q.wait()

    @pl.when(me > 0)
    def _():
        to_right().wait_recv()

        @pl.when(me != half)
        def _():
            first_copy(me).wait_recv()

    @pl.when(me < n - 1)
    def _():
        to_left().wait_recv()

        @pl.when(me != half - 1)
        def _():
            final_copy(me).wait_recv()

    nt = (((1,), (1,)), ((), ()))

    def near(j, c):
        block = me * blocks + j
        rows = pl.ds(pl.multiple_of(j * BLOCK, BLOCK), BLOCK)
        b_prev = jnp.where(block >= 1, 0.0, NEG)
        b_next = jnp.where(block <= total_blocks - 2, 0.0, NEG)
        b_first = jnp.where(block >= 2, 0.0, NEG)
        b_final = jnp.where(block <= total_blocks - 3, 0.0, NEG)
        col = lax.broadcasted_iota(jnp.int32, (BLOCK, 3 * BLOCK), 1)
        b_win = jnp.where(col < BLOCK, b_prev, jnp.where(col >= 2 * BLOCK, b_next, 0.0))
        cole = lax.broadcasted_iota(jnp.int32, (BLOCK, 2 * BLOCK), 1)
        b_end = jnp.where(cole < BLOCK, b_first, b_final)
        for hd in range(heads):
            kc = pl.ds(hd * HEAD_DIM, HEAD_DIM)
            vc = pl.ds(feat + hd * HEAD_DIM, HEAD_DIM)
            qh = q_ref[rows, kc]
            kw = kvp[pl.ds(j, 3), :, kc].reshape(3 * BLOCK, HEAD_DIM)
            vw = kvp[pl.ds(j, 3), :, vc].reshape(3 * BLOCK, HEAD_DIM)
            ke = ends[:, :, kc].reshape(2 * BLOCK, HEAD_DIM)
            ve = ends[:, :, vc].reshape(2 * BLOCK, HEAD_DIM)
            sw = lax.dot_general(qh, kw, nt, preferred_element_type=jnp.float32) * scale + b_win
            se = lax.dot_general(qh, ke, nt, preferred_element_type=jnp.float32) * scale + b_end
            m = jnp.maximum(
                jnp.max(sw, axis=1, keepdims=True), jnp.max(se, axis=1, keepdims=True)
            )
            pw = jnp.exp(sw - m)
            pe = jnp.exp(se - m)
            tot = jnp.sum(pw, axis=1, keepdims=True) + jnp.sum(pe, axis=1, keepdims=True)
            o = jnp.dot(pw.astype(jnp.bfloat16), vw, preferred_element_type=jnp.float32)
            o = o + jnp.dot(pe.astype(jnp.bfloat16), ve, preferred_element_type=jnp.float32)
            m_ref[rows, kc] = jnp.broadcast_to(m, (BLOCK, HEAD_DIM))
            l_ref[rows, kc] = jnp.broadcast_to(tot, (BLOCK, HEAD_DIM))
            acc[rows, kc] = o
        return c

    lax.fori_loop(0, blocks, near, 0)

    def wf_copy(g, c):
        return remote(w_piece(g, c), w_piece(g, c), wf_send.at[c], wf_recv.at[c], me, sib)

    def wy_copy(span):
        return remote(wall.at[across, span], wall.at[across, span], wy_send, wy_recv, pair, h)

    def rand_wait(hd):
        def go(i, c):
            rand_copy(hd, peer(i), me).wait_recv()
            return c

        lax.fori_loop(0, n - 1, go, 0)

    quarter = blocks // 4

    def att_copy(hd, t, g):
        return remote(
            att.at[hd, t], attr.at[hd, g], att_send.at[hd * 4 + t], att_recv.at[hd * 4 + g], me, t
        )

    def places(j):
        s0 = tabs_s[n * 8 + 2 * j, 0]
        s1 = tabs_s[n * 8 + 2 * j + 1, 0]
        return (s0 // slots, lax.rem(s0, slots)), (s1 // slots, lax.rem(s1, slots))

    def gathered(part, j):
        (r0, k0), (r1, k1) = places(j)
        return jnp.concatenate([recvs[part][r0, k0], recvs[part][r1, k1]], axis=0)

    def weigh(hd, j, keys):
        kc = pl.ds(hd * HEAD_DIM, HEAD_DIM)
        rows = pl.ds(pl.multiple_of(j * BLOCK, BLOCK), BLOCK)
        block = me * blocks + j
        n0, n1 = rb_ref[0, j], rb_ref[1, j]

        def clash(x):
            near_by = (x >= block - 1) & (x <= block + 1)
            return near_by | (x == 0) | (x == total_blocks - 1)

        b0 = jnp.where(clash(n0), NEG, 0.0)
        b1 = jnp.where(clash(n1) | (n1 == n0), NEG, 0.0)
        col = lax.broadcasted_iota(jnp.int32, (BLOCK, 2 * BLOCK), 1)
        bias = jnp.where(col < BLOCK, b0, b1)
        s = lax.dot_general(q_ref[rows, kc], keys, nt, preferred_element_type=jnp.float32)
        s = s * scale + bias
        m0 = m_ref[rows, kc]
        m = jnp.maximum(m0, jnp.max(s, axis=1, keepdims=True))
        alpha = jnp.exp(m0 - m)
        p = jnp.exp(s - m)
        tot = l_ref[rows, kc] * alpha + jnp.sum(p, axis=1, keepdims=True)
        return p.astype(jnp.bfloat16), acc[rows, kc] * alpha, tot

    def finish(hd, t, u, p, vals, base, tot):
        o = jnp.dot(p, vals, preferred_element_type=jnp.float32) + base
        att[hd, t, u * BLOCK : (u + 1) * BLOCK, :] = (o / tot).astype(jnp.bfloat16)

    def each_pair(hd, do):
        def one(i, c):
            ts = [2 * lax.rem(h // 2 + 1 + i, 2) + lax.rem(h + v, 2) for v in range(2)]
            for t in ts:
                for u in range(quarter):
                    do(t, u, t * quarter + u)
            if hd is not None:

                @pl.when(i == 0)
                def _():
                    att_copy(hd, ts[0], h).start()

                att_copy(hd, ts[1], h).start()
            return c

        lax.fori_loop(0, 2, one, 0)

    def far(hd):
        def do(t, u, j):
            both = gathered(hd, j)
            p, base, tot = weigh(hd, j, both[:, :HEAD_DIM])
            finish(hd, t, u, p, both[:, HEAD_DIM:], base, tot)

        each_pair(hd, do)

    def last_keys():
        kc = pl.ds(last * HEAD_DIM, HEAD_DIM)

        def do(t, u, j):
            rows = pl.ds(pl.multiple_of(j * BLOCK, BLOCK), BLOCK)
            p, base, tot = weigh(last, j, gathered(last, j))
            p_ref[rows, :] = p
            acc[rows, kc] = base
            l_ref[rows, kc] = tot

        each_pair(None, do)

    def last_values():
        kc = pl.ds(last * HEAD_DIM, HEAD_DIM)

        def do(t, u, j):
            rows = pl.ds(pl.multiple_of(j * BLOCK, BLOCK), BLOCK)
            finish(last, t, u, p_ref[rows, :], gathered(heads, j), acc[rows, kc], l_ref[rows, kc])

        each_pair(last, do)

    tile = 512
    tiles = out_ref.shape[1] // tile
    early = (heads - 1) * HEAD_DIM

    def joined(buf, g):
        return jnp.concatenate([buf[hd, g] for hd in range(heads - 1)], axis=1)

    def project_a(i, c):
        cols = pl.ds(pl.multiple_of(i * tile, tile), tile)
        o = jnp.dot(joined(att, h), wall[h, :early, cols], preferred_element_type=jnp.float32)
        for g in (sib, across, across_sib):
            o = o + jnp.dot(
                joined(attr, g), wall[g, :early, cols], preferred_element_type=jnp.float32
            )
        oacc[:, cols] = o
        return c

    def tail(bufs, cols):
        rows = jnp.concatenate([buf[last, g] for buf, g in bufs], axis=1)
        weights = jnp.concatenate([wall[g, early:, cols] for buf, g in bufs], axis=0)
        return oacc[:, cols] + jnp.dot(rows, weights, preferred_element_type=jnp.float32)

    def project_b(i, c):
        cols = pl.ds(pl.multiple_of(i * tile, tile), tile)
        oacc[:, cols] = tail(((att, h), (attr, sib)), cols)
        return c

    def out_copy(i):
        cols = pl.ds(pl.multiple_of(i * tile, tile), tile)
        return pltpu.make_async_copy(out_v.at[:, cols], out_ref.at[:, cols], out_sem.at[i])

    def project_c(i, c):
        cols = pl.ds(pl.multiple_of(i * tile, tile), tile)
        o = tail(((attr, across), (attr, across_sib)), cols)
        out_v[:, cols] = o.astype(jnp.bfloat16)
        out_copy(i).start()
        return c

    def out_wait(i, c):
        out_copy(i).wait()
        return c

    for hd in range(heads):
        if hd < last:
            wx_copy(across, hd).wait_recv()
            wf_copy(across, hd).start()
        if hd == 0:
            wy_copy(w_span(0)).start()
        if hd == last:
            wy_copy(w_span(last)).wait_recv()
            wf_copy(across, last).start()
            w_own.wait()
            ws_copy.wait_recv()
            for c in range(W_CHUNKS):
                wf_copy(across_sib, c).wait_recv()
            for e in range(last):
                for g in others:
                    att_copy(e, h, g).wait_recv()
            lax.fori_loop(0, tiles, project_a, 0)
        rand_wait(hd)
        if hd < last:
            far(hd)
    last_keys()
    rand_wait(heads)
    last_values()

    att_copy(last, h, sib).wait_recv()
    lax.fori_loop(0, tiles, project_b, 0)
    att_copy(last, h, across).wait_recv()
    att_copy(last, h, across_sib).wait_recv()
    lax.fori_loop(0, tiles, project_c, 0)

    def drain(i, c):
        tab_copy(me, peer(i)).wait_send()
        for hd in range(parts):
            rand_copy(hd, me, peer(i)).wait_send()
        return c

    lax.fori_loop(0, n - 1, drain, 0)

    def from_mates(copy):
        def go(i, c):
            copy(mate(i)).wait_send()
            return c

        lax.fori_loop(0, half - 1, go, 0)

    @pl.when(me == 0)
    def _():
        first_copy(half).wait_send()
        from_mates(first_copy)

    @pl.when(me == n - 1)
    def _():
        final_copy(half - 1).wait_send()
        from_mates(final_copy)

    @pl.when(me == half)
    def _():
        from_mates(first_relay)

    @pl.when(me == half - 1)
    def _():
        from_mates(final_relay)

    @pl.when(me < n - 1)
    def _():
        to_right().wait_send()

    @pl.when(me > 0)
    def _():
        to_left().wait_send()

    for c in range(W_CHUNKS):
        if c < last:
            wx_copy(h, c).wait_send()
        wf_copy(across, c).wait_send()
    wy_copy(w_span(0)).wait_send()
    ws_copy.wait_send()
    for hd in range(heads):
        for t in others:
            att_copy(hd, t, h).wait_send()
    lax.fori_loop(0, tiles, out_wait, 0)


def hand_over(src, dst, sem):
    rows = src.shape[0] // 8
    copies = [
        pltpu.make_async_copy(
            src.at[pl.ds(i * rows, rows)], dst.at[pl.ds(i * rows, rows)], sem.at[i]
        )
        for i in range(8)
    ]
    for copy in copies:
        copy.start()
    for copy in copies:
        copy.wait()


def body(queries, keys_values, rand_blocks, w_out):
    tok_rows, feat = queries.shape
    heads = feat // HEAD_DIM
    blocks = tok_rows // BLOCK
    n = lax.axis_size("seq")
    n_head = lax.axis_size("head")
    entries = rand_blocks.shape[0] * rand_blocks.shape[1]
    slots = max(1, entries // n)
    width = w_out.shape[1]
    kv = keys_values.reshape(blocks, BLOCK, 2, feat)
    anywhere = pl.BlockSpec(memory_space=pl.ANY)
    bf16, f32, i32 = jnp.bfloat16, jnp.float32, jnp.int32
    rows_out = tok_rows // n_head
    dma = pltpu.SemaphoreType.DMA
    mixed = pl.pallas_call(
        functools.partial(kernel, n, slots, blocks, heads),
        out_shape=jax.ShapeDtypeStruct((rows_out, width), bf16),
        in_specs=[anywhere, anywhere, pl.BlockSpec(memory_space=pltpu.SMEM), anywhere],
        out_specs=anywhere,
        scratch_shapes=[
            pltpu.VMEM((tok_rows, feat), bf16),
            pltpu.VMEM((blocks, BLOCK, 2, feat), bf16),
            pltpu.VMEM((blocks, BLOCK, 2 * feat), bf16),
            pltpu.VMEM((8, 128), i32),
            pltpu.VMEM((rows_out, width), bf16),
            dma((2,)),
            dma((width // 512,)),
            pltpu.VMEM((blocks + 2, BLOCK, 2 * feat), bf16),
            pltpu.VMEM((2, BLOCK, 2 * feat), bf16),
            pltpu.VMEM((n * 8 + entries, 128), i32),
            pltpu.SMEM((n * 8 + entries, 128), i32),
            pltpu.VMEM((heads - 1, n, slots, BLOCK, 2 * HEAD_DIM), bf16),
            *[pltpu.VMEM((n, slots, BLOCK, 2 * HEAD_DIM), bf16)] * 3,
            *[pltpu.VMEM((n, slots, BLOCK, HEAD_DIM), bf16)] * 4,
            pltpu.VMEM((tok_rows, HEAD_DIM), bf16),
            pltpu.VMEM((tok_rows, feat), f32),
            pltpu.VMEM((tok_rows, feat), f32),
            pltpu.VMEM((tok_rows, feat), f32),
            pltpu.VMEM((heads, n_head, rows_out, HEAD_DIM), bf16),
            pltpu.VMEM((heads, n_head, rows_out, HEAD_DIM), bf16),
            pltpu.VMEM((n_head, feat, width), bf16),
            pltpu.VMEM((rows_out, width), f32),
            dma((n,)),
            dma((n,)),
            dma,
            dma((2,)),
            dma((2,)),
            dma((n,)),
            dma((n,)),
            dma((2,)),
            dma(((heads + 1) * n,)),
            dma(((heads + 1) * n,)),
            dma,
            dma((W_CHUNKS,)),
            dma((W_CHUNKS,)),
            dma,
            dma,
            dma((W_CHUNKS,)),
            dma((W_CHUNKS,)),
            dma,
            dma,
            dma((heads * n_head,)),
            dma((heads * n_head,)),
        ],
        compiler_params=pltpu.CompilerParams(
            collective_id=0, has_side_effects=True, vmem_limit_bytes=60 * 1024 * 1024
        ),
        cost_estimate=pl.CostEstimate(
            flops=6_000_000_000, bytes_accessed=20_000_000, transcendentals=2_000_000
        ),
    )(queries, kv, rand_blocks.T, w_out)
    return pl.pallas_call(
        hand_over,
        out_shape=jax.ShapeDtypeStruct((rows_out, width), bf16),
        in_specs=[anywhere],
        out_specs=anywhere,
        scratch_shapes=[dma((8,))],
    )(mixed)


def solution(mesh):
    in_specs = (P("seq", "head"), P("seq", None, "head"), P("seq", None), P("head", None))
    out_specs = P(("seq", "head"), None)
    return jax.shard_map(body, mesh=mesh, in_specs=in_specs, out_specs=out_specs, check_vma=False)
```

```python
import functools

import jax
import jax.numpy as jnp
from jax import lax
from jax.experimental import pallas as pl
from jax.experimental.pallas import tpu as pltpu
from jax.sharding import PartitionSpec as P

HEAD_DIM = 128
BLOCK = 64
W_CHUNKS = 4
NEG = -1e30


def kernel(
    n,
    slots,
    blocks,
    heads,
    q_hbm,
    raw_hbm,
    rb_ref,
    w_ref,
    out_ref,
    q_ref,
    raw_ref,
    kv_ref,
    tab_ref,
    out_v,
    in_sem,
    out_sem,
    kvp,
    ends,
    tabs,
    tabs_s,
    stage,
    recv_0,
    recv_1,
    recv_2,
    recv_3,
    recv_4,
    stage_3,
    stage_4,
    p_ref,
    m_ref,
    l_ref,
    acc,
    att,
    attr,
    wall,
    oacc,
    tab_send,
    tab_recv,
    tab_local,
    halo_send,
    halo_recv,
    first_send,
    final_send,
    ends_recv,
    rand_send,
    rand_recv,
    w_local,
    wx_send,
    wx_recv,
    ws_send,
    ws_recv,
    wf_send,
    wf_recv,
    wy_send,
    wy_recv,
    att_send,
    att_recv,
):
    recvs = (recv_0, recv_1, recv_2, recv_3, recv_4)
    stages = (stage.at[0], stage.at[1], stage.at[2], stage_3, stage_4)
    parts = heads + 1
    last = heads - 1
    me = lax.axis_index("seq")
    h = lax.axis_index("head")
    sib = h + 1 - 2 * lax.rem(h, 2)
    across = lax.rem(h + 2, 4)
    across_sib = lax.rem(sib + 2, 4)
    others = (across, across_sib, sib)
    total_blocks = n * blocks
    scale = HEAD_DIM ** (-0.5)
    w_rows = w_ref.shape[0] // W_CHUNKS
    feat = heads * HEAD_DIM

    def remote(src, dst, ssem, rsem, seq, head):
        return pltpu.make_async_remote_copy(
            src_ref=src,
            dst_ref=dst,
            send_sem=ssem,
            recv_sem=rsem,
            device_id=(seq, head),
            device_id_type=pl.DeviceIdType.MESH,
        )

    half = n // 2
    side, place = me // half, lax.rem(me, half)
    pair = me + 1 - 2 * lax.rem(me, 2)

    deep = half // 2
    level, lane = place // 2, lax.rem(place, 2)

    def peer(i):
        over = 1 - lax.rem(i, 2)
        k = (i + 1) // 2
        inward = lax.rem(k, deep)
        facing = inward + (1 - side) * (deep - 1 - 2 * inward)
        to_level = over * facing + (1 - over) * lax.rem(level + inward, deep)
        to_lane = lax.rem(lane + k // deep, 2)
        return lax.rem(side + over, 2) * half + to_level * 2 + to_lane

    def mate(i):
        return side * half + lax.rem(place + 1 + i, half)

    load_raw = pltpu.make_async_copy(raw_hbm, raw_ref, in_sem.at[0])
    load_q = pltpu.make_async_copy(q_hbm, q_ref, in_sem.at[1])
    load_raw.start()
    load_q.start()

    barrier = pltpu.get_barrier_semaphore()

    def greet(i, c):
        pl.semaphore_signal(
            barrier, inc=1, device_id=(peer(i), h), device_id_type=pl.DeviceIdType.MESH
        )
        return c

    lax.fori_loop(0, n - 1, greet, 0)
    for g in others:
        pl.semaphore_signal(barrier, inc=1, device_id=(me, g), device_id_type=pl.DeviceIdType.MESH)
    entries = 2 * blocks
    lanes = lax.broadcasted_iota(jnp.int32, (entries, 128), 1)
    subs = lax.broadcasted_iota(jnp.int32, (entries, 128), 0)
    owner_row = jnp.full((entries, 128), -1, jnp.int32)
    owner_col = jnp.zeros((entries, 128), jnp.int32)
    offset_col = jnp.zeros((entries, 128), jnp.int32)
    for e in range(entries):
        named = rb_ref[e % 2, e // 2]
        owner = named // blocks
        owner_row = jnp.where(lanes == e, owner, owner_row)
        owner_col = jnp.where(subs == e, owner, owner_col)
        offset_col = jnp.where(subs == e, named - owner * blocks, offset_col)
    ahead = jnp.where((owner_row == owner_col) & (lanes < subs), 1, 0)
    slot_col = owner_col * slots + jnp.sum(ahead, axis=1, keepdims=True)
    outgoing = jnp.sum(jnp.where(slot_col == lanes, offset_col, 0), axis=0, keepdims=True)
    tab_ref[...] = jnp.broadcast_to(outgoing, (8, 128))
    tabs[n * 8 : n * 8 + entries, :] = slot_col

    pl.semaphore_wait(barrier, n - 1 + 3)

    def tab_copy(s, dest):
        return remote(
            tab_ref, tabs.at[pl.ds(s * 8, 8)], tab_send.at[dest], tab_recv.at[s], dest, h
        )

    def tab_start(i, c):
        tab_copy(me, peer(i)).start()
        return c

    lax.fori_loop(0, n - 1, tab_start, 0)

    load_raw.wait()

    def unpack(j):
        kv_ref[j, :, :feat] = raw_ref[j, :, 0, :]
        kv_ref[j, :, feat:] = raw_ref[j, :, 1, :]

    unpack(0)
    unpack(blocks - 1)

    def to_right():
        return remote(
            kv_ref.at[blocks - 1], kvp.at[0], halo_send.at[0], halo_recv.at[0], lax.rem(me + 1, n), h
        )

    def to_left():
        return remote(
            kv_ref.at[0],
            kvp.at[blocks + 1],
            halo_send.at[1],
            halo_recv.at[1],
            lax.rem(me + n - 1, n),
            h,
        )

    def first_copy(dest):
        return remote(kv_ref.at[0], ends.at[0], first_send.at[dest], ends_recv.at[0], dest, h)

    def final_copy(dest):
        return remote(kv_ref.at[blocks - 1], ends.at[1], final_send.at[dest], ends_recv.at[1], dest, h)

    def first_relay(dest):
        return remote(ends.at[0], ends.at[0], first_send.at[dest], ends_recv.at[0], dest, h)

    def final_relay(dest):
        return remote(ends.at[1], ends.at[1], final_send.at[dest], ends_recv.at[1], dest, h)

    def to_mates(copy):
        def go(i, c):
            copy(mate(i)).start()
            return c

        lax.fori_loop(0, half - 1, go, 0)

    @pl.when(me == 0)
    def _():
        first_copy(half).start()
        to_mates(first_copy)
        ends[0] = kv_ref[0]
        kvp[0] = jnp.zeros_like(kvp[0])

    @pl.when(me == n - 1)
    def _():
        final_copy(half - 1).start()
        to_mates(final_copy)
        ends[1] = kv_ref[blocks - 1]
        kvp[blocks + 1] = jnp.zeros_like(kvp[0])

    @pl.when(me < n - 1)
    def _():
        to_right().start()

    @pl.when(me > 0)
    def _():
        to_left().start()

    odd = lax.rem(me, 2)

    def w_span(c):
        place_c = c + odd * (W_CHUNKS - 1 - 2 * c)
        return pl.ds(pl.multiple_of(place_c * w_rows, w_rows), w_rows)

    def w_piece(g, c):
        return wall.at[g, w_span(c)]

    def wx_copy(g, c):
        return remote(
            w_ref.at[w_span(c)],
            w_piece(g, c),
            wx_send.at[c],
            wx_recv.at[c],
            me,
            across,
        )

    for c in range(W_CHUNKS - 1):
        wx_copy(h, c).start()

    def tab_wait(i, c):
        tab_copy(peer(i), me).wait_recv()
        return c

    lax.fori_loop(0, n - 1, tab_wait, 0)
    tabs[pl.ds(pl.multiple_of(me * 8, 8), 8), :] = tab_ref[...]
    to_smem = pltpu.make_async_copy(tabs, tabs_s, tab_local)
    to_smem.start()
    to_smem.wait()

    @pl.when(me == half)
    def _():
        first_copy(me).wait_recv()
        to_mates(first_relay)

    @pl.when(me == half - 1)
    def _():
        final_copy(me).wait_recv()
        to_mates(final_relay)

    def rand_copy(hd, s, dest):
        return remote(
            stages[hd].at[dest],
            recvs[hd].at[s],
            rand_send.at[hd * n + dest],
            rand_recv.at[hd * n + s],
            dest,
            h,
        )

    def pick(buf, part, dest):
        hd = min(part, last)
        for k in range(slots):
            block = tabs_s[dest * 8, me * slots + k]
            if part == 0:
                keys = raw_ref[block, :, 0, pl.ds(hd * HEAD_DIM, HEAD_DIM)]
                vals = raw_ref[block, :, 1, pl.ds(hd * HEAD_DIM, HEAD_DIM)]
            else:
                keys = kv_ref[block, :, pl.ds(hd * HEAD_DIM, HEAD_DIM)]
                vals = kv_ref[block, :, pl.ds(feat + hd * HEAD_DIM, HEAD_DIM)]
            if part < last:
                buf[k, :, :HEAD_DIM] = keys
                buf[k, :, HEAD_DIM:] = vals
            else:
                buf[k] = keys if part == last else vals

    for hd in range(parts):

        def rand_start(i, c, hd=hd):
            dest = peer(i)
            pick(stages[hd].at[dest], hd, dest)
            rand_copy(hd, me, dest).start()
            return c

        lax.fori_loop(0, n - 1, rand_start, 0)
        if hd == 0:

            def unpack_one(j, c):
                unpack(j)
                return c

            lax.fori_loop(1, blocks - 1, unpack_one, 0)
    for hd in range(parts):
        pick(recvs[hd].at[me], hd, me)

    w_own = pltpu.make_async_copy(w_ref, wall.at[h], w_local)
    w_own.start()
    ws_copy = remote(w_ref, wall.at[h], ws_send, ws_recv, me, sib)
    ws_copy.start()

    def fill(j, c):
        kvp[j + 1] = kv_ref[j]
        return c

    lax.fori_loop(0, blocks, fill, 0)
    load_q.wait()

    @pl.when(me > 0)
    def _():
        to_right().wait_recv()

        @pl.when(me != half)
        def _():
            first_copy(me).wait_recv()

    @pl.when(me < n - 1)
    def _():
        to_left().wait_recv()

        @pl.when(me != half - 1)
        def _():
            final_copy(me).wait_recv()

    nt = (((1,), (1,)), ((), ()))

    def near(j, c):
        block = me * blocks + j
        rows = pl.ds(pl.multiple_of(j * BLOCK, BLOCK), BLOCK)
        b_prev = jnp.where(block >= 1, 0.0, NEG)
        b_next = jnp.where(block <= total_blocks - 2, 0.0, NEG)
        b_first = jnp.where(block >= 2, 0.0, NEG)
        b_final = jnp.where(block <= total_blocks - 3, 0.0, NEG)
        col = lax.broadcasted_iota(jnp.int32, (BLOCK, 3 * BLOCK), 1)
        b_win = jnp.where(col < BLOCK, b_prev, jnp.where(col >= 2 * BLOCK, b_next, 0.0))
        cole = lax.broadcasted_iota(jnp.int32, (BLOCK, 2 * BLOCK), 1)
        b_end = jnp.where(cole < BLOCK, b_first, b_final)
        for hd in range(heads):
            kc = pl.ds(hd * HEAD_DIM, HEAD_DIM)
            vc = pl.ds(feat + hd * HEAD_DIM, HEAD_DIM)
            qh = q_ref[rows, kc]
            kw = kvp[pl.ds(j, 3), :, kc].reshape(3 * BLOCK, HEAD_DIM)
            vw = kvp[pl.ds(j, 3), :, vc].reshape(3 * BLOCK, HEAD_DIM)
            ke = ends[:, :, kc].reshape(2 * BLOCK, HEAD_DIM)
            ve = ends[:, :, vc].reshape(2 * BLOCK, HEAD_DIM)
            sw = lax.dot_general(qh, kw, nt, preferred_element_type=jnp.float32) * scale + b_win
            se = lax.dot_general(qh, ke, nt, preferred_element_type=jnp.float32) * scale + b_end
            m = jnp.maximum(
                jnp.max(sw, axis=1, keepdims=True), jnp.max(se, axis=1, keepdims=True)
            )
            pw = jnp.exp(sw - m)
            pe = jnp.exp(se - m)
            tot = jnp.sum(pw, axis=1, keepdims=True) + jnp.sum(pe, axis=1, keepdims=True)
            o = jnp.dot(pw.astype(jnp.bfloat16), vw, preferred_element_type=jnp.float32)
            o = o + jnp.dot(pe.astype(jnp.bfloat16), ve, preferred_element_type=jnp.float32)
            m_ref[rows, kc] = jnp.broadcast_to(m, (BLOCK, HEAD_DIM))
            l_ref[rows, kc] = jnp.broadcast_to(tot, (BLOCK, HEAD_DIM))
            acc[rows, kc] = o
        return c

    lax.fori_loop(0, blocks, near, 0)

    def wf_copy(g, c):
        return remote(w_piece(g, c), w_piece(g, c), wf_send.at[c], wf_recv.at[c], me, sib)

    def wy_copy(span):
        return remote(wall.at[across, span], wall.at[across, span], wy_send, wy_recv, pair, h)

    def rand_wait(hd):
        def go(i, c):
            rand_copy(hd, peer(i), me).wait_recv()
            return c

        lax.fori_loop(0, n - 1, go, 0)

    quarter = blocks // 4

    def att_copy(hd, t, g):
        return remote(
            att.at[hd, t], attr.at[hd, g], att_send.at[hd * 4 + t], att_recv.at[hd * 4 + g], me, t
        )

    def places(j):
        s0 = tabs_s[n * 8 + 2 * j, 0]
        s1 = tabs_s[n * 8 + 2 * j + 1, 0]
        return (s0 // slots, lax.rem(s0, slots)), (s1 // slots, lax.rem(s1, slots))

    def gathered(part, j):
        (r0, k0), (r1, k1) = places(j)
        return jnp.concatenate([recvs[part][r0, k0], recvs[part][r1, k1]], axis=0)

    def weigh(hd, j, keys):
        kc = pl.ds(hd * HEAD_DIM, HEAD_DIM)
        rows = pl.ds(pl.multiple_of(j * BLOCK, BLOCK), BLOCK)
        block = me * blocks + j
        n0, n1 = rb_ref[0, j], rb_ref[1, j]

        def clash(x):
            near_by = (x >= block - 1) & (x <= block + 1)
            return near_by | (x == 0) | (x == total_blocks - 1)

        b0 = jnp.where(clash(n0), NEG, 0.0)
        b1 = jnp.where(clash(n1) | (n1 == n0), NEG, 0.0)
        col = lax.broadcasted_iota(jnp.int32, (BLOCK, 2 * BLOCK), 1)
        bias = jnp.where(col < BLOCK, b0, b1)
        s = lax.dot_general(q_ref[rows, kc], keys, nt, preferred_element_type=jnp.float32)
        s = s * scale + bias
        m0 = m_ref[rows, kc]
        m = jnp.maximum(m0, jnp.max(s, axis=1, keepdims=True))
        alpha = jnp.exp(m0 - m)
        p = jnp.exp(s - m)
        tot = l_ref[rows, kc] * alpha + jnp.sum(p, axis=1, keepdims=True)
        return p.astype(jnp.bfloat16), acc[rows, kc] * alpha, tot

    def finish(hd, t, u, p, vals, base, tot):
        o = jnp.dot(p, vals, preferred_element_type=jnp.float32) + base
        att[hd, t, u * BLOCK : (u + 1) * BLOCK, :] = (o / tot).astype(jnp.bfloat16)

    def each_pair(hd, do):
        def one(i, c):
            ts = [2 * lax.rem(h // 2 + 1 + i, 2) + lax.rem(h + v, 2) for v in range(2)]
            for t in ts:
                for u in range(quarter):
                    do(t, u, t * quarter + u)
            if hd is not None:

                @pl.when(i == 0)
                def _():
                    att_copy(hd, ts[0], h).start()

                att_copy(hd, ts[1], h).start()
            return c

        lax.fori_loop(0, 2, one, 0)

    def far(hd):
        def do(t, u, j):
            both = gathered(hd, j)
            p, base, tot = weigh(hd, j, both[:, :HEAD_DIM])
            finish(hd, t, u, p, both[:, HEAD_DIM:], base, tot)

        each_pair(hd, do)

    def last_keys():
        kc = pl.ds(last * HEAD_DIM, HEAD_DIM)

        def do(t, u, j):
            rows = pl.ds(pl.multiple_of(j * BLOCK, BLOCK), BLOCK)
            p, base, tot = weigh(last, j, gathered(last, j))
            p_ref[rows, :] = p
            acc[rows, kc] = base
            l_ref[rows, kc] = tot

        each_pair(None, do)

    def last_values():
        kc = pl.ds(last * HEAD_DIM, HEAD_DIM)

        def do(t, u, j):
            rows = pl.ds(pl.multiple_of(j * BLOCK, BLOCK), BLOCK)
            finish(last, t, u, p_ref[rows, :], gathered(heads, j), acc[rows, kc], l_ref[rows, kc])

        each_pair(last, do)

    tile = 512
    tiles = out_ref.shape[1] // tile
    early = (heads - 1) * HEAD_DIM

    def joined(buf, g):
        return jnp.concatenate([buf[hd, g] for hd in range(heads - 1)], axis=1)

    def project_a(i, c):
        cols = pl.ds(pl.multiple_of(i * tile, tile), tile)
        o = jnp.dot(joined(att, h), wall[h, :early, cols], preferred_element_type=jnp.float32)
        for g in (sib, across, across_sib):
            o = o + jnp.dot(
                joined(attr, g), wall[g, :early, cols], preferred_element_type=jnp.float32
            )
        oacc[:, cols] = o
        return c

    def tail(bufs, cols):
        rows = jnp.concatenate([buf[last, g] for buf, g in bufs], axis=1)
        weights = jnp.concatenate([wall[g, early:, cols] for buf, g in bufs], axis=0)
        return oacc[:, cols] + jnp.dot(rows, weights, preferred_element_type=jnp.float32)

    def project_b(i, c):
        cols = pl.ds(pl.multiple_of(i * tile, tile), tile)
        oacc[:, cols] = tail(((att, h), (attr, sib)), cols)
        return c

    def out_copy(i):
        cols = pl.ds(pl.multiple_of(i * tile, tile), tile)
        return pltpu.make_async_copy(out_v.at[:, cols], out_ref.at[:, cols], out_sem.at[i])

    def project_c(i, c):
        cols = pl.ds(pl.multiple_of(i * tile, tile), tile)
        o = tail(((attr, across), (attr, across_sib)), cols)
        out_v[:, cols] = o.astype(jnp.bfloat16)
        out_copy(i).start()
        return c

    def out_wait(i, c):
        out_copy(i).wait()
        return c

    for hd in range(heads):
        if hd < last:
            wx_copy(across, hd).wait_recv()
            wf_copy(across, hd).start()
        if hd == 0:
            wy_copy(w_span(0)).start()
        if hd == last:
            wy_copy(w_span(last)).wait_recv()
            wf_copy(across, last).start()
            w_own.wait()
            ws_copy.wait_recv()
            for c in range(W_CHUNKS):
                wf_copy(across_sib, c).wait_recv()
            for e in range(last):
                for g in others:
                    att_copy(e, h, g).wait_recv()
            lax.fori_loop(0, tiles, project_a, 0)
        rand_wait(hd)
        if hd < last:
            far(hd)
    last_keys()
    rand_wait(heads)
    last_values()

    att_copy(last, h, sib).wait_recv()
    lax.fori_loop(0, tiles, project_b, 0)
    att_copy(last, h, across).wait_recv()
    att_copy(last, h, across_sib).wait_recv()
    lax.fori_loop(0, tiles, project_c, 0)

    def drain(i, c):
        tab_copy(me, peer(i)).wait_send()
        for hd in range(parts):
            rand_copy(hd, me, peer(i)).wait_send()
        return c

    lax.fori_loop(0, n - 1, drain, 0)

    def from_mates(copy):
        def go(i, c):
            copy(mate(i)).wait_send()
            return c

        lax.fori_loop(0, half - 1, go, 0)

    @pl.when(me == 0)
    def _():
        first_copy(half).wait_send()
        from_mates(first_copy)

    @pl.when(me == n - 1)
    def _():
        final_copy(half - 1).wait_send()
        from_mates(final_copy)

    @pl.when(me == half)
    def _():
        from_mates(first_relay)

    @pl.when(me == half - 1)
    def _():
        from_mates(final_relay)

    @pl.when(me < n - 1)
    def _():
        to_right().wait_send()

    @pl.when(me > 0)
    def _():
        to_left().wait_send()

    for c in range(W_CHUNKS):
        if c < last:
            wx_copy(h, c).wait_send()
        wf_copy(across, c).wait_send()
    wy_copy(w_span(0)).wait_send()
    ws_copy.wait_send()
    for hd in range(heads):
        for t in others:
            att_copy(hd, t, h).wait_send()
    lax.fori_loop(0, tiles, out_wait, 0)


def hand_over(src, dst, held, in_sem, out_sem):
    rows = src.shape[0] // 8

    def arrive(i):
        span = pl.ds(i * rows, rows)
        return pltpu.make_async_copy(src.at[span], held.at[span], in_sem.at[i])

    def leave(i):
        span = pl.ds(i * rows, rows)
        return pltpu.make_async_copy(held.at[span], dst.at[span], out_sem.at[i])

    for i in range(8):
        arrive(i).start()
    for i in range(8):
        arrive(i).wait()
        leave(i).start()
    for i in range(8):
        leave(i).wait()


def body(queries, keys_values, rand_blocks, w_out):
    tok_rows, feat = queries.shape
    heads = feat // HEAD_DIM
    blocks = tok_rows // BLOCK
    n = lax.axis_size("seq")
    n_head = lax.axis_size("head")
    entries = rand_blocks.shape[0] * rand_blocks.shape[1]
    slots = max(1, entries // n)
    width = w_out.shape[1]
    kv = keys_values.reshape(blocks, BLOCK, 2, feat)
    anywhere = pl.BlockSpec(memory_space=pl.ANY)
    bf16, f32, i32 = jnp.bfloat16, jnp.float32, jnp.int32
    rows_out = tok_rows // n_head
    dma = pltpu.SemaphoreType.DMA
    mixed = pl.pallas_call(
        functools.partial(kernel, n, slots, blocks, heads),
        out_shape=jax.ShapeDtypeStruct((rows_out, width), bf16),
        in_specs=[anywhere, anywhere, pl.BlockSpec(memory_space=pltpu.SMEM), anywhere],
        out_specs=anywhere,
        scratch_shapes=[
            pltpu.VMEM((tok_rows, feat), bf16),
            pltpu.VMEM((blocks, BLOCK, 2, feat), bf16),
            pltpu.VMEM((blocks, BLOCK, 2 * feat), bf16),
            pltpu.VMEM((8, 128), i32),
            pltpu.VMEM((rows_out, width), bf16),
            dma((2,)),
            dma((width // 512,)),
            pltpu.VMEM((blocks + 2, BLOCK, 2 * feat), bf16),
            pltpu.VMEM((2, BLOCK, 2 * feat), bf16),
            pltpu.VMEM((n * 8 + entries, 128), i32),
            pltpu.SMEM((n * 8 + entries, 128), i32),
            pltpu.VMEM((heads - 1, n, slots, BLOCK, 2 * HEAD_DIM), bf16),
            *[pltpu.VMEM((n, slots, BLOCK, 2 * HEAD_DIM), bf16)] * 3,
            *[pltpu.VMEM((n, slots, BLOCK, HEAD_DIM), bf16)] * 4,
            pltpu.VMEM((tok_rows, HEAD_DIM), bf16),
            pltpu.VMEM((tok_rows, feat), f32),
            pltpu.VMEM((tok_rows, feat), f32),
            pltpu.VMEM((tok_rows, feat), f32),
            pltpu.VMEM((heads, n_head, rows_out, HEAD_DIM), bf16),
            pltpu.VMEM((heads, n_head, rows_out, HEAD_DIM), bf16),
            pltpu.VMEM((n_head, feat, width), bf16),
            pltpu.VMEM((rows_out, width), f32),
            dma((n,)),
            dma((n,)),
            dma,
            dma((2,)),
            dma((2,)),
            dma((n,)),
            dma((n,)),
            dma((2,)),
            dma(((heads + 1) * n,)),
            dma(((heads + 1) * n,)),
            dma,
            dma((W_CHUNKS,)),
            dma((W_CHUNKS,)),
            dma,
            dma,
            dma((W_CHUNKS,)),
            dma((W_CHUNKS,)),
            dma,
            dma,
            dma((heads * n_head,)),
            dma((heads * n_head,)),
        ],
        compiler_params=pltpu.CompilerParams(
            collective_id=0, has_side_effects=True, vmem_limit_bytes=60 * 1024 * 1024
        ),
        cost_estimate=pl.CostEstimate(
            flops=6_000_000_000, bytes_accessed=20_000_000, transcendentals=2_000_000
        ),
    )(queries, kv, rand_blocks.T, w_out)
    return pl.pallas_call(
        hand_over,
        out_shape=jax.ShapeDtypeStruct((rows_out, width), bf16),
        in_specs=[anywhere],
        out_specs=anywhere,
        scratch_shapes=[pltpu.VMEM((rows_out, width), bf16), dma((8,)), dma((8,))],
    )(mixed)


def solution(mesh):
    in_specs = (P("seq", "head"), P("seq", None, "head"), P("seq", None), P("head", None))
    out_specs = P(("seq", "head"), None)
    return jax.shard_map(body, mesh=mesh, in_specs=in_specs, out_specs=out_specs, check_vma=False)
```

```python
import functools

import jax
import jax.numpy as jnp
from jax import lax
from jax.experimental import pallas as pl
from jax.experimental.pallas import tpu as pltpu
from jax.sharding import PartitionSpec as P

HEAD_DIM = 128
BLOCK = 64
W_CHUNKS = 4
NEG = -1e30


def kernel(
    n,
    slots,
    blocks,
    heads,
    q_hbm,
    raw_hbm,
    rb_ref,
    w_ref,
    out_ref,
    q_ref,
    raw_ref,
    kv_ref,
    tab_ref,
    in_sem,
    kvp,
    ends,
    tabs,
    tabs_s,
    stage,
    recv_0,
    recv_1,
    recv_2,
    recv_3,
    recv_4,
    stage_3,
    stage_4,
    p_ref,
    m_ref,
    l_ref,
    acc,
    att,
    attr,
    wall,
    oacc,
    tab_send,
    tab_recv,
    tab_local,
    halo_send,
    halo_recv,
    first_send,
    final_send,
    ends_recv,
    rand_send,
    rand_recv,
    w_local,
    wx_send,
    wx_recv,
    ws_send,
    ws_recv,
    wf_send,
    wf_recv,
    wy_send,
    wy_recv,
    att_send,
    att_recv,
):
    recvs = (recv_0, recv_1, recv_2, recv_3, recv_4)
    stages = (stage.at[0], stage.at[1], stage.at[2], stage_3, stage_4)
    parts = heads + 1
    last = heads - 1
    me = lax.axis_index("seq")
    h = lax.axis_index("head")
    sib = h + 1 - 2 * lax.rem(h, 2)
    across = lax.rem(h + 2, 4)
    across_sib = lax.rem(sib + 2, 4)
    others = (across, across_sib, sib)
    total_blocks = n * blocks
    scale = HEAD_DIM ** (-0.5)
    w_rows = w_ref.shape[0] // W_CHUNKS
    feat = heads * HEAD_DIM

    def remote(src, dst, ssem, rsem, seq, head):
        return pltpu.make_async_remote_copy(
            src_ref=src,
            dst_ref=dst,
            send_sem=ssem,
            recv_sem=rsem,
            device_id=(seq, head),
            device_id_type=pl.DeviceIdType.MESH,
        )

    half = n // 2
    side, place = me // half, lax.rem(me, half)
    pair = me + 1 - 2 * lax.rem(me, 2)

    deep = half // 2
    level, lane = place // 2, lax.rem(place, 2)

    def peer(i):
        over = 1 - lax.rem(i, 2)
        k = (i + 1) // 2
        inward = lax.rem(k, deep)
        facing = inward + (1 - side) * (deep - 1 - 2 * inward)
        to_level = over * facing + (1 - over) * lax.rem(level + inward, deep)
        to_lane = lax.rem(lane + k // deep, 2)
        return lax.rem(side + over, 2) * half + to_level * 2 + to_lane

    def mate(i):
        return side * half + lax.rem(place + 1 + i, half)

    load_raw = pltpu.make_async_copy(raw_hbm, raw_ref, in_sem.at[0])
    load_q = pltpu.make_async_copy(q_hbm, q_ref, in_sem.at[1])
    load_raw.start()
    load_q.start()

    barrier = pltpu.get_barrier_semaphore()

    def greet(i, c):
        pl.semaphore_signal(
            barrier, inc=1, device_id=(peer(i), h), device_id_type=pl.DeviceIdType.MESH
        )
        return c

    lax.fori_loop(0, n - 1, greet, 0)
    for g in others:
        pl.semaphore_signal(barrier, inc=1, device_id=(me, g), device_id_type=pl.DeviceIdType.MESH)
    entries = 2 * blocks
    lanes = lax.broadcasted_iota(jnp.int32, (entries, 128), 1)
    subs = lax.broadcasted_iota(jnp.int32, (entries, 128), 0)
    owner_row = jnp.full((entries, 128), -1, jnp.int32)
    owner_col = jnp.zeros((entries, 128), jnp.int32)
    offset_col = jnp.zeros((entries, 128), jnp.int32)
    for e in range(entries):
        named = rb_ref[e % 2, e // 2]
        owner = named // blocks
        owner_row = jnp.where(lanes == e, owner, owner_row)
        owner_col = jnp.where(subs == e, owner, owner_col)
        offset_col = jnp.where(subs == e, named - owner * blocks, offset_col)
    ahead = jnp.where((owner_row == owner_col) & (lanes < subs), 1, 0)
    slot_col = owner_col * slots + jnp.sum(ahead, axis=1, keepdims=True)
    outgoing = jnp.sum(jnp.where(slot_col == lanes, offset_col, 0), axis=0, keepdims=True)
    tab_ref[...] = jnp.broadcast_to(outgoing, (8, 128))
    tabs[n * 8 : n * 8 + entries, :] = slot_col

    pl.semaphore_wait(barrier, n - 1 + 3)

    def tab_copy(s, dest):
        return remote(
            tab_ref, tabs.at[pl.ds(s * 8, 8)], tab_send.at[dest], tab_recv.at[s], dest, h
        )

    def tab_start(i, c):
        tab_copy(me, peer(i)).start()
        return c

    lax.fori_loop(0, n - 1, tab_start, 0)

    load_raw.wait()

    def unpack(j):
        kv_ref[j, :, :feat] = raw_ref[j, :, 0, :]
        kv_ref[j, :, feat:] = raw_ref[j, :, 1, :]

    unpack(0)
    unpack(blocks - 1)

    def to_right():
        return remote(
            kv_ref.at[blocks - 1], kvp.at[0], halo_send.at[0], halo_recv.at[0], lax.rem(me + 1, n), h
        )

    def to_left():
        return remote(
            kv_ref.at[0],
            kvp.at[blocks + 1],
            halo_send.at[1],
            halo_recv.at[1],
            lax.rem(me + n - 1, n),
            h,
        )

    def first_copy(dest):
        return remote(kv_ref.at[0], ends.at[0], first_send.at[dest], ends_recv.at[0], dest, h)

    def final_copy(dest):
        return remote(kv_ref.at[blocks - 1], ends.at[1], final_send.at[dest], ends_recv.at[1], dest, h)

    def first_relay(dest):
        return remote(ends.at[0], ends.at[0], first_send.at[dest], ends_recv.at[0], dest, h)

    def final_relay(dest):
        return remote(ends.at[1], ends.at[1], final_send.at[dest], ends_recv.at[1], dest, h)

    def to_mates(copy):
        def go(i, c):
            copy(mate(i)).start()
            return c

        lax.fori_loop(0, half - 1, go, 0)

    @pl.when(me == 0)
    def _():
        first_copy(half).start()
        to_mates(first_copy)
        ends[0] = kv_ref[0]
        kvp[0] = jnp.zeros_like(kvp[0])

    @pl.when(me == n - 1)
    def _():
        final_copy(half - 1).start()
        to_mates(final_copy)
        ends[1] = kv_ref[blocks - 1]
        kvp[blocks + 1] = jnp.zeros_like(kvp[0])

    @pl.when(me < n - 1)
    def _():
        to_right().start()

    @pl.when(me > 0)
    def _():
        to_left().start()

    odd = lax.rem(me, 2)

    def w_span(c):
        place_c = c + odd * (W_CHUNKS - 1 - 2 * c)
        return pl.ds(pl.multiple_of(place_c * w_rows, w_rows), w_rows)

    def w_piece(g, c):
        return wall.at[g, w_span(c)]

    def wx_copy(g, c):
        return remote(
            w_ref.at[w_span(c)],
            w_piece(g, c),
            wx_send.at[c],
            wx_recv.at[c],
            me,
            across,
        )

    for c in range(W_CHUNKS - 1):
        wx_copy(h, c).start()

    def tab_wait(i, c):
        tab_copy(peer(i), me).wait_recv()
        return c

    lax.fori_loop(0, n - 1, tab_wait, 0)
    tabs[pl.ds(pl.multiple_of(me * 8, 8), 8), :] = tab_ref[...]
    to_smem = pltpu.make_async_copy(tabs, tabs_s, tab_local)
    to_smem.start()
    to_smem.wait()

    @pl.when(me == half)
    def _():
        first_copy(me).wait_recv()
        to_mates(first_relay)

    @pl.when(me == half - 1)
    def _():
        final_copy(me).wait_recv()
        to_mates(final_relay)

    def rand_copy(hd, s, dest):
        return remote(
            stages[hd].at[dest],
            recvs[hd].at[s],
            rand_send.at[hd * n + dest],
            rand_recv.at[hd * n + s],
            dest,
            h,
        )

    def pick(buf, part, dest):
        hd = min(part, last)
        for k in range(slots):
            block = tabs_s[dest * 8, me * slots + k]
            if part == 0:
                keys = raw_ref[block, :, 0, pl.ds(hd * HEAD_DIM, HEAD_DIM)]
                vals = raw_ref[block, :, 1, pl.ds(hd * HEAD_DIM, HEAD_DIM)]
            else:
                keys = kv_ref[block, :, pl.ds(hd * HEAD_DIM, HEAD_DIM)]
                vals = kv_ref[block, :, pl.ds(feat + hd * HEAD_DIM, HEAD_DIM)]
            if part < last:
                buf[k, :, :HEAD_DIM] = keys
                buf[k, :, HEAD_DIM:] = vals
            else:
                buf[k] = keys if part == last else vals

    for hd in range(parts):

        def rand_start(i, c, hd=hd):
            dest = peer(i)
            pick(stages[hd].at[dest], hd, dest)
            rand_copy(hd, me, dest).start()
            return c

        lax.fori_loop(0, n - 1, rand_start, 0)
        if hd == 0:

            def unpack_one(j, c):
                unpack(j)
                return c

            lax.fori_loop(1, blocks - 1, unpack_one, 0)
    for hd in range(parts):
        pick(recvs[hd].at[me], hd, me)

    w_own = pltpu.make_async_copy(w_ref, wall.at[h], w_local)
    w_own.start()
    ws_copy = remote(w_ref, wall.at[h], ws_send, ws_recv, me, sib)
    ws_copy.start()

    def fill(j, c):
        kvp[j + 1] = kv_ref[j]
        return c

    lax.fori_loop(0, blocks, fill, 0)
    load_q.wait()

    @pl.when(me > 0)
    def _():
        to_right().wait_recv()

        @pl.when(me != half)
        def _():
            first_copy(me).wait_recv()

    @pl.when(me < n - 1)
    def _():
        to_left().wait_recv()

        @pl.when(me != half - 1)
        def _():
            final_copy(me).wait_recv()

    nt = (((1,), (1,)), ((), ()))

    def near(j, c):
        block = me * blocks + j
        rows = pl.ds(pl.multiple_of(j * BLOCK, BLOCK), BLOCK)
        b_prev = jnp.where(block >= 1, 0.0, NEG)
        b_next = jnp.where(block <= total_blocks - 2, 0.0, NEG)
        b_first = jnp.where(block >= 2, 0.0, NEG)
        b_final = jnp.where(block <= total_blocks - 3, 0.0, NEG)
        col = lax.broadcasted_iota(jnp.int32, (BLOCK, 3 * BLOCK), 1)
        b_win = jnp.where(col < BLOCK, b_prev, jnp.where(col >= 2 * BLOCK, b_next, 0.0))
        cole = lax.broadcasted_iota(jnp.int32, (BLOCK, 2 * BLOCK), 1)
        b_end = jnp.where(cole < BLOCK, b_first, b_final)
        for hd in range(heads):
            kc = pl.ds(hd * HEAD_DIM, HEAD_DIM)
            vc = pl.ds(feat + hd * HEAD_DIM, HEAD_DIM)
            qh = q_ref[rows, kc]
            kw = kvp[pl.ds(j, 3), :, kc].reshape(3 * BLOCK, HEAD_DIM)
            vw = kvp[pl.ds(j, 3), :, vc].reshape(3 * BLOCK, HEAD_DIM)
            ke = ends[:, :, kc].reshape(2 * BLOCK, HEAD_DIM)
            ve = ends[:, :, vc].reshape(2 * BLOCK, HEAD_DIM)
            sw = lax.dot_general(qh, kw, nt, preferred_element_type=jnp.float32) * scale + b_win
            se = lax.dot_general(qh, ke, nt, preferred_element_type=jnp.float32) * scale + b_end
            m = jnp.maximum(
                jnp.max(sw, axis=1, keepdims=True), jnp.max(se, axis=1, keepdims=True)
            )
            pw = jnp.exp(sw - m)
            pe = jnp.exp(se - m)
            tot = jnp.sum(pw, axis=1, keepdims=True) + jnp.sum(pe, axis=1, keepdims=True)
            o = jnp.dot(pw.astype(jnp.bfloat16), vw, preferred_element_type=jnp.float32)
            o = o + jnp.dot(pe.astype(jnp.bfloat16), ve, preferred_element_type=jnp.float32)
            m_ref[rows, kc] = jnp.broadcast_to(m, (BLOCK, HEAD_DIM))
            l_ref[rows, kc] = jnp.broadcast_to(tot, (BLOCK, HEAD_DIM))
            acc[rows, kc] = o
        return c

    lax.fori_loop(0, blocks, near, 0)

    def wf_copy(g, c):
        return remote(w_piece(g, c), w_piece(g, c), wf_send.at[c], wf_recv.at[c], me, sib)

    def wy_copy(span):
        return remote(wall.at[across, span], wall.at[across, span], wy_send, wy_recv, pair, h)

    def rand_wait(hd):
        def go(i, c):
            rand_copy(hd, peer(i), me).wait_recv()
            return c

        lax.fori_loop(0, n - 1, go, 0)

    quarter = blocks // 4

    def att_copy(hd, t, g):
        return remote(
            att.at[hd, t], attr.at[hd, g], att_send.at[hd * 4 + t], att_recv.at[hd * 4 + g], me, t
        )

    def places(j):
        s0 = tabs_s[n * 8 + 2 * j, 0]
        s1 = tabs_s[n * 8 + 2 * j + 1, 0]
        return (s0 // slots, lax.rem(s0, slots)), (s1 // slots, lax.rem(s1, slots))

    def gathered(part, j):
        (r0, k0), (r1, k1) = places(j)
        return jnp.concatenate([recvs[part][r0, k0], recvs[part][r1, k1]], axis=0)

    def weigh(hd, j, keys):
        kc = pl.ds(hd * HEAD_DIM, HEAD_DIM)
        rows = pl.ds(pl.multiple_of(j * BLOCK, BLOCK), BLOCK)
        block = me * blocks + j
        n0, n1 = rb_ref[0, j], rb_ref[1, j]

        def clash(x):
            near_by = (x >= block - 1) & (x <= block + 1)
            return near_by | (x == 0) | (x == total_blocks - 1)

        b0 = jnp.where(clash(n0), NEG, 0.0)
        b1 = jnp.where(clash(n1) | (n1 == n0), NEG, 0.0)
        col = lax.broadcasted_iota(jnp.int32, (BLOCK, 2 * BLOCK), 1)
        bias = jnp.where(col < BLOCK, b0, b1)
        s = lax.dot_general(q_ref[rows, kc], keys, nt, preferred_element_type=jnp.float32)
        s = s * scale + bias
        m0 = m_ref[rows, kc]
        m = jnp.maximum(m0, jnp.max(s, axis=1, keepdims=True))
        alpha = jnp.exp(m0 - m)
        p = jnp.exp(s - m)
        tot = l_ref[rows, kc] * alpha + jnp.sum(p, axis=1, keepdims=True)
        return p.astype(jnp.bfloat16), acc[rows, kc] * alpha, tot

    def finish(hd, t, u, p, vals, base, tot):
        o = jnp.dot(p, vals, preferred_element_type=jnp.float32) + base
        att[hd, t, u * BLOCK : (u + 1) * BLOCK, :] = (o / tot).astype(jnp.bfloat16)

    def each_pair(hd, do):
        def one(i, c):
            ts = [2 * lax.rem(h // 2 + 1 + i, 2) + lax.rem(h + v, 2) for v in range(2)]
            for t in ts:
                for u in range(quarter):
                    do(t, u, t * quarter + u)
            if hd is not None:

                @pl.when(i == 0)
                def _():
                    att_copy(hd, ts[0], h).start()

                att_copy(hd, ts[1], h).start()
            return c

        lax.fori_loop(0, 2, one, 0)

    def far(hd):
        def do(t, u, j):
            both = gathered(hd, j)
            p, base, tot = weigh(hd, j, both[:, :HEAD_DIM])
            finish(hd, t, u, p, both[:, HEAD_DIM:], base, tot)

        each_pair(hd, do)

    def last_keys():
        kc = pl.ds(last * HEAD_DIM, HEAD_DIM)

        def do(t, u, j):
            rows = pl.ds(pl.multiple_of(j * BLOCK, BLOCK), BLOCK)
            p, base, tot = weigh(last, j, gathered(last, j))
            p_ref[rows, :] = p
            acc[rows, kc] = base
            l_ref[rows, kc] = tot

        each_pair(None, do)

    def last_values():
        kc = pl.ds(last * HEAD_DIM, HEAD_DIM)

        def do(t, u, j):
            rows = pl.ds(pl.multiple_of(j * BLOCK, BLOCK), BLOCK)
            finish(last, t, u, p_ref[rows, :], gathered(heads, j), acc[rows, kc], l_ref[rows, kc])

        each_pair(last, do)

    tile = 512
    tiles = out_ref.shape[1] // tile
    early = (heads - 1) * HEAD_DIM

    def joined(buf, g):
        return jnp.concatenate([buf[hd, g] for hd in range(heads - 1)], axis=1)

    def project_a(i, c):
        cols = pl.ds(pl.multiple_of(i * tile, tile), tile)
        o = jnp.dot(joined(att, h), wall[h, :early, cols], preferred_element_type=jnp.float32)
        for g in (sib, across, across_sib):
            o = o + jnp.dot(
                joined(attr, g), wall[g, :early, cols], preferred_element_type=jnp.float32
            )
        oacc[:, cols] = o
        return c

    def tail(bufs, cols):
        rows = jnp.concatenate([buf[last, g] for buf, g in bufs], axis=1)
        weights = jnp.concatenate([wall[g, early:, cols] for buf, g in bufs], axis=0)
        return oacc[:, cols] + jnp.dot(rows, weights, preferred_element_type=jnp.float32)

    def project_b(i, c):
        cols = pl.ds(pl.multiple_of(i * tile, tile), tile)
        oacc[:, cols] = tail(((att, h), (attr, sib)), cols)
        return c

    def project_c(i, c):
        cols = pl.ds(pl.multiple_of(i * tile, tile), tile)
        o = tail(((attr, across), (attr, across_sib)), cols)
        out_ref[:, cols] = o.astype(jnp.bfloat16)
        return c

    for hd in range(heads):
        if hd < last:
            wx_copy(across, hd).wait_recv()
            wf_copy(across, hd).start()
        if hd == 0:
            wy_copy(w_span(0)).start()
        if hd == last:
            wy_copy(w_span(last)).wait_recv()
            wf_copy(across, last).start()
            w_own.wait()
            ws_copy.wait_recv()
            for c in range(W_CHUNKS):
                wf_copy(across_sib, c).wait_recv()
            for e in range(last):
                for g in others:
                    att_copy(e, h, g).wait_recv()
            lax.fori_loop(0, tiles, project_a, 0)
        rand_wait(hd)
        if hd < last:
            far(hd)
    last_keys()
    rand_wait(heads)
    last_values()

    att_copy(last, h, sib).wait_recv()
    lax.fori_loop(0, tiles, project_b, 0)
    att_copy(last, h, across).wait_recv()
    att_copy(last, h, across_sib).wait_recv()
    lax.fori_loop(0, tiles, project_c, 0)

    def drain(i, c):
        tab_copy(me, peer(i)).wait_send()
        for hd in range(parts):
            rand_copy(hd, me, peer(i)).wait_send()
        return c

    lax.fori_loop(0, n - 1, drain, 0)

    def from_mates(copy):
        def go(i, c):
            copy(mate(i)).wait_send()
            return c

        lax.fori_loop(0, half - 1, go, 0)

    @pl.when(me == 0)
    def _():
        first_copy(half).wait_send()
        from_mates(first_copy)

    @pl.when(me == n - 1)
    def _():
        final_copy(half - 1).wait_send()
        from_mates(final_copy)

    @pl.when(me == half)
    def _():
        from_mates(first_relay)

    @pl.when(me == half - 1)
    def _():
        from_mates(final_relay)

    @pl.when(me < n - 1)
    def _():
        to_right().wait_send()

    @pl.when(me > 0)
    def _():
        to_left().wait_send()

    for c in range(W_CHUNKS):
        if c < last:
            wx_copy(h, c).wait_send()
        wf_copy(across, c).wait_send()
    wy_copy(w_span(0)).wait_send()
    ws_copy.wait_send()
    for hd in range(heads):
        for t in others:
            att_copy(hd, t, h).wait_send()


def hand_over(src, dst, sem):
    rows = src.shape[0] // 8

    def leave(i):
        span = pl.ds(i * rows, rows)
        return pltpu.make_async_copy(src.at[span], dst.at[span], sem.at[i])

    for i in range(8):
        leave(i).start()
    for i in range(8):
        leave(i).wait()


def body(queries, keys_values, rand_blocks, w_out):
    tok_rows, feat = queries.shape
    heads = feat // HEAD_DIM
    blocks = tok_rows // BLOCK
    n = lax.axis_size("seq")
    n_head = lax.axis_size("head")
    entries = rand_blocks.shape[0] * rand_blocks.shape[1]
    slots = max(1, entries // n)
    width = w_out.shape[1]
    kv = keys_values.reshape(blocks, BLOCK, 2, feat)
    anywhere = pl.BlockSpec(memory_space=pl.ANY)
    vmem = pl.BlockSpec(memory_space=pltpu.VMEM)
    bf16, f32, i32 = jnp.bfloat16, jnp.float32, jnp.int32
    rows_out = tok_rows // n_head
    dma = pltpu.SemaphoreType.DMA
    mixed = pl.pallas_call(
        functools.partial(kernel, n, slots, blocks, heads),
        out_shape=pltpu.VMEM((rows_out, width), bf16),
        in_specs=[anywhere, anywhere, pl.BlockSpec(memory_space=pltpu.SMEM), anywhere],
        out_specs=vmem,
        scratch_shapes=[
            pltpu.VMEM((tok_rows, feat), bf16),
            pltpu.VMEM((blocks, BLOCK, 2, feat), bf16),
            pltpu.VMEM((blocks, BLOCK, 2 * feat), bf16),
            pltpu.VMEM((8, 128), i32),
            dma((2,)),
            pltpu.VMEM((blocks + 2, BLOCK, 2 * feat), bf16),
            pltpu.VMEM((2, BLOCK, 2 * feat), bf16),
            pltpu.VMEM((n * 8 + entries, 128), i32),
            pltpu.SMEM((n * 8 + entries, 128), i32),
            pltpu.VMEM((heads - 1, n, slots, BLOCK, 2 * HEAD_DIM), bf16),
            *[pltpu.VMEM((n, slots, BLOCK, 2 * HEAD_DIM), bf16)] * 3,
            *[pltpu.VMEM((n, slots, BLOCK, HEAD_DIM), bf16)] * 4,
            pltpu.VMEM((tok_rows, HEAD_DIM), bf16),
            pltpu.VMEM((tok_rows, feat), f32),
            pltpu.VMEM((tok_rows, feat), f32),
            pltpu.VMEM((tok_rows, feat), f32),
            pltpu.VMEM((heads, n_head, rows_out, HEAD_DIM), bf16),
            pltpu.VMEM((heads, n_head, rows_out, HEAD_DIM), bf16),
            pltpu.VMEM((n_head, feat, width), bf16),
            pltpu.VMEM((rows_out, width), f32),
            dma((n,)),
            dma((n,)),
            dma,
            dma((2,)),
            dma((2,)),
            dma((n,)),
            dma((n,)),
            dma((2,)),
            dma(((heads + 1) * n,)),
            dma(((heads + 1) * n,)),
            dma,
            dma((W_CHUNKS,)),
            dma((W_CHUNKS,)),
            dma,
            dma,
            dma((W_CHUNKS,)),
            dma((W_CHUNKS,)),
            dma,
            dma,
            dma((heads * n_head,)),
            dma((heads * n_head,)),
        ],
        compiler_params=pltpu.CompilerParams(
            collective_id=0, has_side_effects=True, vmem_limit_bytes=56 * 1024 * 1024
        ),
        cost_estimate=pl.CostEstimate(
            flops=6_000_000_000, bytes_accessed=20_000_000, transcendentals=2_000_000
        ),
    )(queries, kv, rand_blocks.T, w_out)
    return pl.pallas_call(
        hand_over,
        out_shape=jax.ShapeDtypeStruct((rows_out, width), bf16),
        in_specs=[vmem],
        out_specs=anywhere,
        scratch_shapes=[dma((8,))],
    )(mixed)


def solution(mesh):
    in_specs = (P("seq", "head"), P("seq", None, "head"), P("seq", None), P("head", None))
    out_specs = P(("seq", "head"), None)
    return jax.shard_map(body, mesh=mesh, in_specs=in_specs, out_specs=out_specs, check_vma=False)
```
